128 devices in a mesh: pipe: 16 (over y_lo, x, core), tensor: 8 (over y_hi, z).
Axes of the slice: x: 4, y: 4 (y_hi: 2, y_lo: 2; y = y_hi * 2 + y_lo), z: 4, core: 2. Of those that a mesh axis runs over, the one named last changes fastest.
Arguments:
- forward_in: bfloat16 [16, 128, 4096], P('pipe', 'tensor'), may hold values from -21 to 21
- entering: bfloat16 [128, 4096], P('tensor'), may hold values from -21 to 21
- backward_in: bfloat16 [16, 128, 4096], P('pipe', 'tensor'), may hold values from -1.5 to 1.5
- loss_grad: bfloat16 [128, 4096], P('tensor'), may hold values from -1.5 to 1.5
- stashed: bfloat16 [16, 2, 128, 4096], P('pipe'), may hold values from -21 to 21
- norm_gain: float32 [16, 4096], P('pipe'), may hold values from 0.5 to 1.5
- w_query: bfloat16 [16, 4096, 4096], P('pipe', None, 'tensor'), may hold values from -0.09375 to 0.09375
- key_projection: bfloat16 [16, 4096, 1024], P('pipe', None, 'tensor'), may hold values from -0.09375 to 0.09375
- value_projection: bfloat16 [16, 4096, 1024], P('pipe', None, 'tensor'), may hold values from -0.09375 to 0.09375
- w_out: bfloat16 [16, 4096, 4096], P('pipe', 'tensor'), may hold values from -0.25 to 0.25
Outputs:
- forward_out: bfloat16 [2, 16, 128, 4096], P(None, 'pipe', 'tensor')
- backward_out: bfloat16 [2, 16, 128, 4096], P(None, 'pipe', 'tensor')
- grad_query: bfloat16 [16, 4096, 4096], P('pipe', None, 'tensor')
- key_weight_gradient: bfloat16 [16, 4096, 1024], P('pipe', None, 'tensor')
- value_weight_gradient: bfloat16 [16, 4096, 1024], P('pipe', None, 'tensor')
- grad_out: bfloat16 [16, 4096, 4096], P('pipe', 'tensor')
- grad_gain: float32 [16, 4096], P('pipe')
The draws below stay inside these ranges and needn't reach their ends.
All inputs are finite; a program needn't handle non-finite values.
Results may differ from the reference program's by a relative error of at most 0.029.
Values may be sent and summed in bfloat16 or wider, within the bound.
No kernel may reach another device: no remote copies, remote signals or barrier semaphores. Data moves between devices by JAX's collectives and lax.ppermute only.
A program may use at most 128 MiB of HBM per device.

```python
import math
import jax
import jax.numpy as jnp
from jax import lax

MODEL_WIDTH = 4096
QUERY_HEAD_COUNT = 32
KEY_VALUE_HEADS = 8
HEAD_DIMENSION = 128
MICRO_TOKENS = 128
TICKS = 2
RELAY_SECTIONS = 16
HEAD_GROUPS = 8


def spread_rows(base_key, leading, row_low, row_high, normal_part):
    row_key, col_key, normal_key = jax.random.split(base_key, 3)
    row_scale = jnp.exp(jax.random.uniform(row_key, leading + (MICRO_TOKENS, 1), jnp.float32, math.log(row_low), math.log(row_high)))
    col_scale = jnp.exp(jax.random.uniform(col_key, (MODEL_WIDTH,), jnp.float32, math.log(0.3), math.log(3.0)))
    gaussian = jnp.clip(jax.random.normal(normal_key, leading + (MICRO_TOKENS, MODEL_WIDTH), jnp.float32), -3.0, 3.0)
    mixed = normal_part * gaussian * row_scale * col_scale
    return mixed.astype(jnp.bfloat16)


def draw_forward_in(key, part):
    key = jax.random.fold_in(key, 11)
    return spread_rows(key, (RELAY_SECTIONS,), 0.3, 3.0, 0.6)


def draw_entering(key, part):
    key = jax.random.fold_in(key, 23)
    return spread_rows(key, (), 0.3, 3.0, 0.6)


def draw_stashed(key, part):
    key = jax.random.fold_in(key, 37)
    return spread_rows(key, (RELAY_SECTIONS, TICKS), 0.3, 3.0, 0.6)


def shard_levels(rng, extent, shards, smallest, top_value):
    def one(dim, blocks):
        steps = jax.random.uniform(jax.random.fold_in(jax.random.fold_in(rng, 6), dim), (blocks,), jnp.float32, smallest / len(shards), top_value / len(shards))
        return jnp.repeat(jnp.exp(steps), extent[dim] // blocks).reshape((-1,) + (1,) * (len(extent) - dim - 1))

    factor_of = one(*shards[0])
    for cut in shards[1:]:
        factor_of = factor_of * one(*cut)
    return factor_of


def noise(rng, extent, scale, most, cuts=(), kind=jnp.bfloat16):
    factor_of = shard_levels(rng, extent, cuts, -0.22, 0.18) if cuts else 1.0
    drawn = jax.random.normal(rng, extent, jnp.float32) * scale * factor_of
    return jnp.minimum(jnp.maximum(drawn, -most), most).astype(kind)


def setup_inputs(seed: int = 0) -> dict:
    arg_keys = jax.random.split(jax.random.key(seed), 11)
    forward_in = draw_forward_in(jax.random.fold_in(arg_keys[10], 71), 0)
    entering = draw_entering(jax.random.fold_in(arg_keys[10], 71), 0)
    backward_in = noise(arg_keys[2], (RELAY_SECTIONS, MICRO_TOKENS, MODEL_WIDTH), 0.1, 1.5, ((0, 16), (1, 8)))
    loss_grad = noise(arg_keys[3], (MICRO_TOKENS, MODEL_WIDTH), 0.1, 1.5, ((0, 8),))
    stashed = draw_stashed(jax.random.fold_in(arg_keys[10], 71), 0)
    norm_gain = jnp.clip(1.0 + 0.1 * jax.random.normal(arg_keys[5], (RELAY_SECTIONS, MODEL_WIDTH), jnp.float32), 0.5, 1.5)
    w_query = noise(arg_keys[6], (RELAY_SECTIONS, MODEL_WIDTH, QUERY_HEAD_COUNT * HEAD_DIMENSION), MODEL_WIDTH ** -0.5, 0.09375, ((0, 16), (2, 8)))
    key_projection = noise(arg_keys[7], (RELAY_SECTIONS, MODEL_WIDTH, KEY_VALUE_HEADS * HEAD_DIMENSION), MODEL_WIDTH ** -0.5, 0.09375, ((0, 16), (2, 8)))
    value_projection = noise(arg_keys[8], (RELAY_SECTIONS, MODEL_WIDTH, KEY_VALUE_HEADS * HEAD_DIMENSION), MODEL_WIDTH ** -0.5, 0.09375, ((0, 16), (2, 8)))
    w_out = noise(arg_keys[9], (RELAY_SECTIONS, QUERY_HEAD_COUNT * HEAD_DIMENSION, MODEL_WIDTH), (4 * HEAD_DIMENSION) ** -0.5, 0.25, ((0, 16), (1, 8)))
    return {"forward_in": forward_in, "entering": entering, "backward_in": backward_in, "loss_grad": loss_grad, "stashed": stashed, "norm_gain": norm_gain, "w_query": w_query, "key_projection": key_projection, "value_projection": value_projection, "w_out": w_out}


EPSILON = 1e-05
ROPE_BASE = 10000.0

def rope_tables():
    positions = jnp.arange(MICRO_TOKENS, dtype=jnp.float32)[:, None]
    exponents = jnp.arange(HEAD_DIMENSION // 2, dtype=jnp.float32) * (2.0 / HEAD_DIMENSION)
    angles = positions * (ROPE_BASE ** (-exponents))[None, :]
    angles = jnp.concatenate([angles, angles], axis=1)
    return (jnp.cos(angles), jnp.sin(angles))

def apply_rotary(values, cosine_table, sine_table):
    half_size = values.shape[-1] // 2
    turned = jnp.concatenate([-values[..., half_size:], values[..., :half_size]], axis=-1)
    return values * cosine_table[:, None, :] + turned * sine_table[:, None, :]

def reverse_rotary(gradient, cosine_table, sine_table):
    half_size = gradient.shape[-1] // 2
    scaled = gradient * sine_table[:, None, :]
    turned = jnp.concatenate([scaled[..., half_size:], -scaled[..., :half_size]], axis=-1)
    return gradient * cosine_table[:, None, :] + turned

def attend(layer_in, gain_row, w_query, key_projection, value_projection, cosine_table, sine_table):
    heads_per_group = QUERY_HEAD_COUNT // KEY_VALUE_HEADS
    wide_in = layer_in.astype(jnp.float32)
    inverse = lax.rsqrt(lax.optimization_barrier(jnp.mean(wide_in * wide_in, axis=-1, keepdims=True)) + EPSILON)
    normalized_input = (wide_in * inverse * gain_row[None, :]).astype(jnp.bfloat16)
    projected_queries = jnp.dot(normalized_input, w_query, preferred_element_type=jnp.float32).reshape(MICRO_TOKENS, QUERY_HEAD_COUNT, HEAD_DIMENSION)
    projected_queries = apply_rotary(projected_queries, cosine_table, sine_table).astype(jnp.bfloat16).reshape(MICRO_TOKENS, KEY_VALUE_HEADS, heads_per_group, HEAD_DIMENSION)
    projected_keys = jnp.dot(normalized_input, key_projection, preferred_element_type=jnp.float32).reshape(MICRO_TOKENS, KEY_VALUE_HEADS, HEAD_DIMENSION)
    projected_keys = apply_rotary(projected_keys, cosine_table, sine_table).astype(jnp.bfloat16)
    projected_values = jnp.dot(normalized_input, value_projection, preferred_element_type=jnp.float32).astype(jnp.bfloat16).reshape(MICRO_TOKENS, KEY_VALUE_HEADS, HEAD_DIMENSION)
    scores = jnp.einsum('qhgd,khd->hgqk', projected_queries.astype(jnp.float32), projected_keys.astype(jnp.float32)) * HEAD_DIMENSION ** (-0.5)
    causal = jnp.arange(MICRO_TOKENS)[:, None] >= jnp.arange(MICRO_TOKENS)[None, :]
    exponent_terms = jnp.where(causal, jnp.exp(scores), 0.0)
    probability = exponent_terms / lax.optimization_barrier(jnp.sum(exponent_terms, axis=-1, keepdims=True))
    weights = probability.astype(jnp.bfloat16)
    attended = jnp.einsum('hgqk,khd->qhgd', weights.astype(jnp.float32), projected_values.astype(jnp.float32))
    attended = attended.astype(jnp.bfloat16).reshape(MICRO_TOKENS, QUERY_HEAD_COUNT * HEAD_DIMENSION)
    return (wide_in, inverse, normalized_input, projected_queries, projected_keys, projected_values, probability, weights, attended)

def section_forward(layer_in, gain_row, w_query, key_projection, value_projection, w_out, cosine_table, sine_table):
    pieces = attend(layer_in, gain_row, w_query, key_projection, value_projection, cosine_table, sine_table)
    attended = pieces[8]
    lane_width = QUERY_HEAD_COUNT * HEAD_DIMENSION // HEAD_GROUPS
    summed = jnp.zeros((MICRO_TOKENS, MODEL_WIDTH), jnp.float32)
    for lane_index in range(HEAD_GROUPS):
        first_col = lane_index * lane_width
        partial_term = jnp.dot(attended[:, first_col:first_col + lane_width], w_out[first_col:first_col + lane_width], preferred_element_type=jnp.float32)
        summed = summed + lax.optimization_barrier(partial_term.astype(jnp.bfloat16)).astype(jnp.float32)
    return (pieces[0] + summed).astype(jnp.bfloat16)

def section_backward(stash_in, grad_rows, gain_row, w_query, key_projection, value_projection, w_out, cosine_table, sine_table):
    wide_in, inverse, normalized_input, projected_queries, projected_keys, projected_values, probability, weights, attended = attend(stash_in, gain_row, w_query, key_projection, value_projection, cosine_table, sine_table)
    heads_per_group = QUERY_HEAD_COUNT // KEY_VALUE_HEADS
    attended_gradient = jnp.dot(grad_rows, w_out.T, preferred_element_type=jnp.float32).astype(jnp.bfloat16)
    grad_w_out = jnp.dot(attended.T, grad_rows, preferred_element_type=jnp.float32)
    group_gradients = attended_gradient.reshape(MICRO_TOKENS, KEY_VALUE_HEADS, heads_per_group, HEAD_DIMENSION).astype(jnp.float32)
    value_weight_gradient = jnp.einsum('hgqk,qhgd->khd', weights.astype(jnp.float32), group_gradients)
    grad_probability = jnp.einsum('qhgd,khd->hgqk', group_gradients, projected_values.astype(jnp.float32))
    row_terms = lax.optimization_barrier(jnp.sum(grad_probability * probability, axis=-1, keepdims=True))
    grad_scores = (probability * (grad_probability - row_terms) * HEAD_DIMENSION ** (-0.5)).astype(jnp.bfloat16).astype(jnp.float32)
    grad_query = jnp.einsum('hgqk,khd->qhgd', grad_scores, projected_keys.astype(jnp.float32)).reshape(MICRO_TOKENS, QUERY_HEAD_COUNT, HEAD_DIMENSION)
    key_weight_gradient = jnp.einsum('hgqk,qhgd->khd', grad_scores, projected_queries.astype(jnp.float32))
    grad_query = reverse_rotary(grad_query, cosine_table, sine_table).astype(jnp.bfloat16).reshape(MICRO_TOKENS, QUERY_HEAD_COUNT * HEAD_DIMENSION)
    key_weight_gradient = reverse_rotary(key_weight_gradient, cosine_table, sine_table).astype(jnp.bfloat16).reshape(MICRO_TOKENS, KEY_VALUE_HEADS * HEAD_DIMENSION)
    value_weight_gradient = value_weight_gradient.astype(jnp.bfloat16).reshape(MICRO_TOKENS, KEY_VALUE_HEADS * HEAD_DIMENSION)
    grad_w_query = jnp.dot(normalized_input.T, grad_query, preferred_element_type=jnp.float32)
    grad_w_key = jnp.dot(normalized_input.T, key_weight_gradient, preferred_element_type=jnp.float32)
    grad_w_value = jnp.dot(normalized_input.T, value_weight_gradient, preferred_element_type=jnp.float32)
    query_width = QUERY_HEAD_COUNT * HEAD_DIMENSION // HEAD_GROUPS
    key_feature_width = KEY_VALUE_HEADS * HEAD_DIMENSION // HEAD_GROUPS
    grad_normed = jnp.zeros((MICRO_TOKENS, MODEL_WIDTH), jnp.float32)
    for lane_index in range(HEAD_GROUPS):
        query_start = lane_index * query_width
        key_start = lane_index * key_feature_width
        partial_term = jnp.dot(grad_query[:, query_start:query_start + query_width], w_query[:, query_start:query_start + query_width].T, preferred_element_type=jnp.float32)
        partial_term = partial_term + jnp.dot(key_weight_gradient[:, key_start:key_start + key_feature_width], key_projection[:, key_start:key_start + key_feature_width].T, preferred_element_type=jnp.float32)
        partial_term = partial_term + jnp.dot(value_weight_gradient[:, key_start:key_start + key_feature_width], value_projection[:, key_start:key_start + key_feature_width].T, preferred_element_type=jnp.float32)
        grad_normed = grad_normed + lax.optimization_barrier(partial_term.astype(jnp.bfloat16)).astype(jnp.float32)
    grad_gain = lax.optimization_barrier(jnp.sum(grad_normed * wide_in * inverse, axis=0))
    scaled_grad = grad_normed * gain_row[None, :]
    grad_in = grad_rows.astype(jnp.float32) + inverse * scaled_grad - wide_in * inverse ** 3 * lax.optimization_barrier(jnp.mean(scaled_grad * wide_in, axis=-1, keepdims=True))
    return (grad_in.astype(jnp.bfloat16), (grad_w_query, grad_w_key, grad_w_value, grad_w_out, grad_gain))

def reference(forward_in, entering, backward_in, loss_grad, stashed, norm_gain, w_query, key_projection, value_projection, w_out):
    cosine_table, sine_table = rope_tables()

    def layer(section_index, layer_in):
        return section_forward(layer_in, norm_gain[section_index], w_query[section_index], key_projection[section_index], value_projection[section_index], w_out[section_index], cosine_table, sine_table)

    def layer_grad(section_index, stash_in, grad_rows):
        return section_backward(stash_in, grad_rows, norm_gain[section_index], w_query[section_index], key_projection[section_index], value_projection[section_index], w_out[section_index], cosine_table, sine_table)
    first_out = [layer(section_index, forward_in[section_index]) for section_index in range(RELAY_SECTIONS)]
    second_in = [entering] + first_out[:-1]
    second_out = [layer(section_index, second_in[section_index]) for section_index in range(RELAY_SECTIONS)]
    first_back = [None] * RELAY_SECTIONS
    second_back = [None] * RELAY_SECTIONS
    totals = [None] * RELAY_SECTIONS
    for section_index in range(RELAY_SECTIONS - 1, -1, -1):
        first_grad_in, first_terms = layer_grad(section_index, stashed[RELAY_SECTIONS - 1 - section_index, 0], backward_in[section_index])
        if section_index == RELAY_SECTIONS - 1:
            arriving = loss_grad
        else:
            arriving = first_back[section_index + 1]
        second_grad_in, second_terms = layer_grad(section_index, stashed[RELAY_SECTIONS - 1 - section_index, 1], arriving)
        first_back[section_index] = first_grad_in
        second_back[section_index] = second_grad_in
        totals[section_index] = [first_terms[index_term] + second_terms[index_term] for index_term in range(5)]
    forward_out = jnp.stack([jnp.stack(first_out), jnp.stack(second_out)])
    backward_out = jnp.stack([jnp.stack(first_back), jnp.stack(second_back)])
    grad_query = jnp.stack([entry_list[0] for entry_list in totals]).astype(jnp.bfloat16)
    key_weight_gradient = jnp.stack([entry_list[1] for entry_list in totals]).astype(jnp.bfloat16)
    value_weight_gradient = jnp.stack([entry_list[2] for entry_list in totals]).astype(jnp.bfloat16)
    grad_out = jnp.stack([entry_list[3] for entry_list in totals]).astype(jnp.bfloat16)
    grad_gain = jnp.stack([entry_list[4] for entry_list in totals])
    return (forward_out, backward_out, grad_query, key_weight_gradient, value_weight_gradient, grad_out, grad_gain)
```

```python
import jax
import jax.numpy as jnp
from jax import lax
from jax.sharding import PartitionSpec as P

HEAD_DIMENSION = 128


EPSILON = 1e-05
ROPE_BASE = 10000.0


def shifted(x, axis, by):
    peers = lax.axis_size(axis)
    pairs = [(i, i + by) for i in range(peers) if 0 <= i + by < peers]
    return lax.ppermute(x, axis, pairs)


def rope_tables(token_count, head_size):
    positions = jnp.arange(token_count, dtype=jnp.float32)[:, None]
    exponents = jnp.arange(head_size // 2, dtype=jnp.float32) * (2.0 / head_size)
    angles = positions * (ROPE_BASE ** (-exponents))[None, :]
    angles = jnp.concatenate([angles, angles], axis=1)
    return (jnp.cos(angles), jnp.sin(angles))


def apply_rotary(values, cosine_table, sine_table):
    half_size = values.shape[-1] // 2
    turned = jnp.concatenate([-values[..., half_size:], values[..., :half_size]], axis=-1)
    return values * cosine_table[:, None, :] + turned * sine_table[:, None, :]


def reverse_rotary(gradient, cosine_table, sine_table):
    half_size = gradient.shape[-1] // 2
    scaled = gradient * sine_table[:, None, :]
    turned = jnp.concatenate([scaled[..., half_size:], -scaled[..., :half_size]], axis=-1)
    return gradient * cosine_table[:, None, :] + turned


def own_rows(full_rows, lane_index, shard_rows):
    return lax.dynamic_slice_in_dim(full_rows, lane_index * shard_rows, shard_rows, 0)


def attend(layer_in, gain_row, w_query, key_projection, value_projection, cosine_table, sine_table):
    token_count = layer_in.shape[0]
    head_size = cosine_table.shape[1]
    query_heads = w_query.shape[1] // head_size
    key_heads = key_projection.shape[1] // head_size
    heads_per_group = query_heads // key_heads
    wide_in = layer_in.astype(jnp.float32)
    inverse = lax.rsqrt(jnp.mean(wide_in * wide_in, axis=-1, keepdims=True) + EPSILON)
    normalized_input = (wide_in * inverse * gain_row[None, :]).astype(jnp.bfloat16)
    projected_queries = jnp.dot(
        normalized_input, w_query, preferred_element_type=jnp.float32
    ).reshape(token_count, query_heads, head_size)
    projected_queries = (
        apply_rotary(projected_queries, cosine_table, sine_table)
        .astype(jnp.bfloat16)
        .reshape(token_count, key_heads, heads_per_group, head_size)
    )
    projected_keys = jnp.dot(
        normalized_input, key_projection, preferred_element_type=jnp.float32
    ).reshape(token_count, key_heads, head_size)
    projected_keys = apply_rotary(projected_keys, cosine_table, sine_table).astype(jnp.bfloat16)
    projected_values = (
        jnp.dot(normalized_input, value_projection, preferred_element_type=jnp.float32)
        .astype(jnp.bfloat16)
        .reshape(token_count, key_heads, head_size)
    )
    scores = jnp.einsum(
        "qhgd,khd->hgqk", projected_queries, projected_keys, preferred_element_type=jnp.float32
    ) * head_size ** (-0.5)
    causal = jnp.arange(token_count)[:, None] >= jnp.arange(token_count)[None, :]
    exponent_terms = jnp.where(causal, jnp.exp(scores), 0.0)
    probability = exponent_terms / jnp.sum(exponent_terms, axis=-1, keepdims=True)
    weights = probability.astype(jnp.bfloat16)
    attended = jnp.einsum(
        "hgqk,khd->qhgd", weights, projected_values, preferred_element_type=jnp.float32
    )
    attended = attended.astype(jnp.bfloat16).reshape(token_count, query_heads * head_size)
    return (
        wide_in,
        inverse,
        normalized_input,
        projected_queries,
        projected_keys,
        projected_values,
        probability,
        weights,
        attended,
    )


def gathered(rows):
    peers = lax.axis_size("tensor")
    copies = jnp.broadcast_to(rows[None], (peers,) + rows.shape)
    return lax.all_to_all(copies, "tensor", 0, 0).reshape(peers * rows.shape[0], rows.shape[1])


def scattered_sum(term):
    peers = lax.axis_size("tensor")
    parts = lax.all_to_all(term.reshape(peers, -1, term.shape[1]), "tensor", 0, 0)
    return jnp.sum(parts.astype(jnp.float32), axis=0)


def section_forward(layer_in, own_in, gain_row, weights_all, cosine_table, sine_table):
    w_query, key_projection, value_projection, w_out = weights_all
    pieces = attend(
        layer_in, gain_row, w_query, key_projection, value_projection, cosine_table, sine_table
    )
    partial_term = jnp.dot(pieces[8], w_out, preferred_element_type=jnp.float32)
    summed = scattered_sum(partial_term.astype(jnp.bfloat16))
    return (own_in.astype(jnp.float32) + summed).astype(jnp.bfloat16)


def section_backward(
    pieces, own_stash, grad_rows, own_grad, gain_row, weights_all, cosine_table, sine_table
):
    w_query, key_projection, value_projection, w_out = weights_all
    (
        wide_in,
        inverse,
        normalized_input,
        projected_queries,
        projected_keys,
        projected_values,
        probability,
        weights,
        attended,
    ) = pieces
    token_count = wide_in.shape[0]
    head_size = cosine_table.shape[1]
    key_heads = projected_keys.shape[1]
    heads_per_group = projected_queries.shape[2]
    contract_last = (((1,), (1,)), ((), ()))
    attended_gradient = lax.dot_general(
        grad_rows, w_out, contract_last, preferred_element_type=jnp.float32
    ).astype(jnp.bfloat16)
    group_gradients = attended_gradient.reshape(token_count, key_heads, heads_per_group, head_size)
    value_grad = jnp.einsum(
        "hgqk,qhgd->khd", weights, group_gradients, preferred_element_type=jnp.float32
    )
    grad_probability = jnp.einsum(
        "qhgd,khd->hgqk", group_gradients, projected_values, preferred_element_type=jnp.float32
    )
    row_terms = jnp.sum(grad_probability * probability, axis=-1, keepdims=True)
    grad_scores = (probability * (grad_probability - row_terms) * head_size ** (-0.5)).astype(
        jnp.bfloat16
    )
    query_grad = jnp.einsum(
        "hgqk,khd->qhgd", grad_scores, projected_keys, preferred_element_type=jnp.float32
    )
    query_grad = query_grad.reshape(token_count, key_heads * heads_per_group, head_size)
    key_grad = jnp.einsum(
        "hgqk,qhgd->khd", grad_scores, projected_queries, preferred_element_type=jnp.float32
    )
    query_grad = (
        reverse_rotary(query_grad, cosine_table, sine_table)
        .astype(jnp.bfloat16)
        .reshape(token_count, -1)
    )
    key_grad = (
        reverse_rotary(key_grad, cosine_table, sine_table)
        .astype(jnp.bfloat16)
        .reshape(token_count, -1)
    )
    value_grad = value_grad.astype(jnp.bfloat16).reshape(token_count, -1)
    partial_term = lax.dot_general(
        query_grad, w_query, contract_last, preferred_element_type=jnp.float32
    )
    partial_term = partial_term + lax.dot_general(
        key_grad, key_projection, contract_last, preferred_element_type=jnp.float32
    )
    partial_term = partial_term + lax.dot_general(
        value_grad, value_projection, contract_last, preferred_element_type=jnp.float32
    )
    rounded = partial_term.astype(jnp.bfloat16)
    gain_part = jnp.sum(rounded.astype(jnp.float32) * wide_in * inverse, axis=0)
    grad_normed = scattered_sum(rounded)
    own_wide = own_stash.astype(jnp.float32)
    own_inverse = lax.rsqrt(jnp.mean(own_wide * own_wide, axis=-1, keepdims=True) + EPSILON)
    scaled_grad = grad_normed * gain_row[None, :]
    grad_in = (
        own_grad.astype(jnp.float32)
        + own_inverse * scaled_grad
        - own_wide * own_inverse**3 * jnp.mean(scaled_grad * own_wide, axis=-1, keepdims=True)
    )
    return (
        grad_in.astype(jnp.bfloat16),
        gain_part,
        (normalized_input, query_grad, key_grad, value_grad, attended),
    )


def mirrored(rows):
    sections = lax.axis_size("pipe")
    peers = lax.axis_size("tensor")
    half = rows.shape[0] // 2
    near, far = [], []
    for section in range(sections):
        for lane in range(peers):
            here = section * peers + lane
            there = (sections - 1 - section) * peers
            near.append((here, there + lane))
            far.append((here, there + (lane ^ peers // 2)))
    return jnp.concatenate(
        [
            lax.ppermute(rows[:half], ("pipe", "tensor"), near),
            lax.ppermute(rows[half:], ("pipe", "tensor"), far),
        ]
    )


def per_device(
    forward_in,
    entering,
    backward_in,
    loss_grad,
    stashed,
    norm_gain,
    w_query,
    key_projection,
    value_projection,
    w_out,
):
    sections = lax.axis_size("pipe")
    section_index = lax.axis_index("pipe")
    lane_index = lax.axis_index("tensor")
    shard_rows = forward_in.shape[1]
    token_count = stashed.shape[2]
    gain_row = norm_gain[0]
    weights_all = (w_query[0], key_projection[0], value_projection[0], w_out[0])
    cosine_table, sine_table = rope_tables(token_count, HEAD_DIMENSION)
    contract_first = (((0,), (0,)), ((), ()))

    def recompute(rows):
        return attend(rows, gain_row, *weights_all[:3], cosine_table, sine_table)

    def weight_gradient(left, right):
        both = lax.dot_general(
            jnp.concatenate(left),
            jnp.concatenate(right),
            contract_first,
            preferred_element_type=jnp.float32,
        )
        return both.astype(jnp.bfloat16)[None]

    saved = (mirrored(stashed[0, 0]), mirrored(stashed[0, 1]))
    own_saved = [own_rows(rows, lane_index, shard_rows) for rows in saved]
    first_in = gathered(forward_in[0])
    first_grad = gathered(backward_in[0])
    first_own = section_forward(
        first_in, forward_in[0], gain_row, weights_all, cosine_table, sine_table
    )
    second_own_in = jnp.where(section_index == 0, entering, shifted(first_own, "pipe", 1))
    second_in = gathered(second_own_in)
    first_back, first_gain, first_terms = section_backward(
        recompute(saved[0]),
        own_saved[0],
        first_grad,
        backward_in[0],
        gain_row,
        weights_all,
        cosine_table,
        sine_table,
    )
    second_own_grad = jnp.where(
        section_index == sections - 1, loss_grad, shifted(first_back, "pipe", -1)
    )
    second_grad = gathered(second_own_grad)
    second_own = section_forward(
        second_in, second_own_in, gain_row, weights_all, cosine_table, sine_table
    )
    second_back, second_gain, second_terms = section_backward(
        recompute(saved[1]),
        own_saved[1],
        second_grad,
        second_own_grad,
        gain_row,
        weights_all,
        cosine_table,
        sine_table,
    )
    forward_out = jnp.stack([first_own, second_own])[:, None]
    backward_out = jnp.stack([first_back, second_back])[:, None]
    normed = (first_terms[0], second_terms[0])
    grad_query = weight_gradient(normed, (first_terms[1], second_terms[1]))
    key_weight_gradient = weight_gradient(normed, (first_terms[2], second_terms[2]))
    value_weight_gradient = weight_gradient(normed, (first_terms[3], second_terms[3]))
    grad_out = weight_gradient(
        (first_terms[4], second_terms[4]), (first_grad, second_grad)
    )
    gain_parts = gathered((first_gain + second_gain)[None])
    grad_gain = jnp.sum(gain_parts, axis=0)[None]
    return (
        forward_out,
        backward_out,
        grad_query,
        key_weight_gradient,
        value_weight_gradient,
        grad_out,
        grad_gain,
    )


def solution(mesh):
    in_specs = (
        P("pipe", "tensor", None),
        P("tensor", None),
        P("pipe", "tensor", None),
        P("tensor", None),
        P("pipe", None, None, None),
        P("pipe", None),
        P("pipe", None, "tensor"),
        P("pipe", None, "tensor"),
        P("pipe", None, "tensor"),
        P("pipe", "tensor", None),
    )
    out_specs = (
        P(None, "pipe", "tensor", None),
        P(None, "pipe", "tensor", None),
        P("pipe", None, "tensor"),
        P("pipe", None, "tensor"),
        P("pipe", None, "tensor"),
        P("pipe", "tensor", None),
        P("pipe", None),
    )
    return jax.shard_map(
        per_device, mesh=mesh, in_specs=in_specs, out_specs=out_specs, check_vma=False
    )
```

```python
import functools

import jax
import jax.numpy as jnp
import numpy as np
from jax import lax
from jax.experimental import pallas as pl
from jax.experimental.pallas import tpu as pltpu
from jax.sharding import PartitionSpec as P

HEAD = 128
EPSILON = 1e-05
ROPE_BASE = 10000.0
CHUNK = 512
VMEM_BYTES = 24 * 1024 * 1024
SHARD = 16
RING = 4
WHOLE = pl.BlockSpec(memory_space=pltpu.VMEM)

NN = (((1,), (0,)), ((), ()))
NT = (((1,), (1,)), ((), ()))
TN = (((0,), (0,)), ((), ()))


def dot(left, right, dims):
    return lax.dot_general(left, right, dims, preferred_element_type=jnp.float32)


def row_tables(token_count):
    lane = lax.axis_index("tensor")
    flip, ahead = np.meshgrid(np.arange(2), np.arange(RING), indexing="ij")
    blocks = ((lane // RING) ^ flip) * RING + (lane + ahead) % RING
    rows = blocks.reshape(-1, 1) * SHARD + np.arange(token_count // blocks.size)
    positions = rows.reshape(-1).astype(jnp.float32)
    exponents = np.arange(HEAD // 2, dtype=np.float32) * np.float32(2.0 / HEAD)
    angles = positions[:, None] * (np.float32(ROPE_BASE) ** (-exponents))[None, :]
    cosine, sine = jnp.cos(angles), jnp.sin(angles)
    return (
        jnp.concatenate([cosine, cosine], axis=1),
        jnp.concatenate([-sine, sine], axis=1),
        (positions[:, None] >= positions[None, :]).astype(jnp.float32),
    )


def rotated(values, cosine, signed_sine):
    return values * cosine + pltpu.roll(values, HEAD // 2, 1) * signed_sine


def rotated_back(values, cosine, signed_sine):
    return values * cosine - pltpu.roll(values, HEAD // 2, 1) * signed_sine


def stacked_heads(wide):
    return jnp.concatenate(
        [wide[:, first : first + HEAD] for first in range(0, wide.shape[1], HEAD)], axis=0
    )


def side_by_side(stacked, tokens):
    return jnp.concatenate(
        [stacked[first : first + tokens] for first in range(0, stacked.shape[0], tokens)], axis=1
    )


def columns(refs, part):
    if len(refs) == 2:
        return jnp.concatenate([ref[:, part] for ref in refs], axis=0)
    pieces = [ref[:SHARD, part] for ref in refs] + [ref[SHARD:, part] for ref in refs]
    return jnp.concatenate(pieces, axis=0)


def attend(x_ref, gain_ref, wq_ref, wk_ref, wv_ref, tables, normed_ref=None):
    cos_ref, sin_ref, mask_ref = tables
    tokens, width = cos_ref.shape[0], wq_ref.shape[0]
    squares = jnp.zeros((tokens, HEAD), jnp.float32)
    for first in range(0, width, HEAD):
        block = columns(x_ref, slice(first, first + HEAD)).astype(jnp.float32)
        squares = squares + block * block
    inverse = lax.rsqrt(jnp.sum(squares, axis=1, keepdims=True) * (1.0 / width) + EPSILON)
    queries = jnp.zeros((tokens, wq_ref.shape[1]), jnp.float32)
    pair = jnp.zeros((tokens, 2 * HEAD), jnp.float32)
    for first in range(0, width, CHUNK):
        part = slice(first, first + CHUNK)
        normed = (
            columns(x_ref, part).astype(jnp.float32) * inverse * gain_ref[:, part]
        ).astype(jnp.bfloat16)
        if normed_ref is not None:
            normed_ref[:, part] = normed
        queries = queries + dot(normed, wq_ref[part, :], NN)
        both = jnp.concatenate([wk_ref[part, :], wv_ref[part, :]], axis=1)
        pair = pair + dot(normed, both, NN)
    cosine, sine = cos_ref[...], sin_ref[...]
    query = jnp.concatenate(
        [
            rotated(queries[:, first : first + HEAD], cosine, sine).astype(jnp.bfloat16)
            for first in range(0, queries.shape[1], HEAD)
        ],
        axis=0,
    )
    key = rotated(pair[:, :HEAD], cosine, sine).astype(jnp.bfloat16)
    value = pair[:, HEAD:].astype(jnp.bfloat16)
    scores = dot(query, key, NT) * HEAD ** (-0.5)
    causal = jnp.concatenate([mask_ref[...]] * (scores.shape[0] // tokens), axis=0) > 0.0
    terms = jnp.where(causal, jnp.exp(scores), 0.0)
    probability = terms / jnp.sum(terms, axis=1, keepdims=True)
    attended = dot(probability.astype(jnp.bfloat16), value, NN).astype(jnp.bfloat16)
    return inverse, query, key, value, probability, side_by_side(attended, tokens)


def forward_kernel(*refs):
    x_refs, (gain_ref, wq_ref, wk_ref, wv_ref, wo_ref) = refs[:RING], refs[RING : RING + 5]
    tables, (near_ref, far_ref) = refs[RING + 5 : RING + 8], refs[RING + 8 :]
    half = near_ref.shape[0]
    attended = attend(x_refs, gain_ref, wq_ref, wk_ref, wv_ref, tables)[5]
    for first in range(0, wo_ref.shape[1], CHUNK):
        part = slice(first, first + CHUNK)
        term = dot(attended, wo_ref[:, part], NN).astype(jnp.bfloat16)
        near_ref[:, part] = term[:half]
        far_ref[:, part] = term[half:]


def recompute_kernel(*refs):
    x_refs, (gain_ref, wq_ref, wk_ref, wv_ref) = refs[:RING], refs[RING : RING + 4]
    tables, outs = refs[RING + 4 : RING + 7], refs[RING + 7 :]
    (
        normed_ref,
        inverse_ref,
        query_ref,
        key_ref,
        value_ref,
        probability_ref,
        attended_ref,
    ) = outs
    inverse, query, key, value, probability, attended = attend(
        x_refs, gain_ref, wq_ref, wk_ref, wv_ref, tables, normed_ref
    )
    inverse_ref[...] = jnp.broadcast_to(inverse, inverse_ref.shape)
    query_ref[...] = query
    key_ref[...] = key
    value_ref[...] = value
    probability_ref[...] = probability
    attended_ref[...] = attended


def backward_kernel(*refs):
    grad_refs, x_refs, refs = refs[:2], refs[2 : 2 + RING], refs[2 + RING :]
    inverse_ref, query_ref, key_ref, value_ref, probability_ref = refs[:5]
    wq_ref, wk_ref, wv_ref, wo_ref = refs[5:9]
    (cos_ref, sin_ref), rest = refs[9:11], refs[11:]
    term_refs, rest = rest[-4 - RING : -4], rest[: -4 - RING] + rest[-4:]
    gain_out_ref, query_grad_ref, key_grad_ref, value_grad_ref = rest[-4:]
    earlier_gain_ref = rest[0] if len(rest) > 4 else None
    tokens, width = cos_ref.shape[0], wq_ref.shape[0]
    grad_attended = jnp.zeros((tokens, wo_ref.shape[0]), jnp.float32)
    for first in range(0, width, CHUNK):
        part = slice(first, first + CHUNK)
        grad_attended = grad_attended + dot(columns(grad_refs, part), wo_ref[:, part], NT)
    grads = stacked_heads(grad_attended.astype(jnp.bfloat16))
    probability = probability_ref[...]
    key, value, query = key_ref[...], value_ref[...], query_ref[...]
    grad_probability = dot(grads, value, NT)
    row_terms = jnp.sum(grad_probability * probability, axis=1, keepdims=True)
    grad_scores = (
        probability * (grad_probability - row_terms) * HEAD ** (-0.5)
    ).astype(jnp.bfloat16)
    cosine, sine = cos_ref[...], sin_ref[...]
    raw = dot(grad_scores, key, NN)
    query_grad = jnp.concatenate(
        [
            rotated_back(raw[first : first + tokens], cosine, sine).astype(jnp.bfloat16)
            for first in range(0, raw.shape[0], tokens)
        ],
        axis=1,
    )
    key_grad = rotated_back(dot(grad_scores, query, TN), cosine, sine).astype(jnp.bfloat16)
    value_grad = dot(probability.astype(jnp.bfloat16), grads, TN).astype(jnp.bfloat16)
    query_grad_ref[...] = query_grad
    key_grad_ref[...] = key_grad
    value_grad_ref[...] = value_grad
    pair_grad = jnp.concatenate([key_grad, value_grad], axis=1)
    inverse = inverse_ref[:, :1]
    gains = []
    for first in range(0, width, CHUNK):
        part = slice(first, first + CHUNK)
        both = jnp.concatenate([wk_ref[part, :], wv_ref[part, :]], axis=1)
        term = dot(query_grad, wq_ref[part, :], NT) + dot(pair_grad, both, NT)
        term = term.astype(jnp.bfloat16)
        for ahead, term_ref in enumerate(term_refs):
            for flip in range(2):
                start = (flip * RING + ahead) * SHARD
                rows = slice(flip * SHARD, flip * SHARD + SHARD)
                term_ref[rows, part] = term[start : start + SHARD]
        gains.append(
            jnp.sum(
                term.astype(jnp.float32) * columns(x_refs, part).astype(jnp.float32) * inverse,
                axis=0,
                keepdims=True,
            )
        )
    gain = jnp.concatenate(gains, axis=0)
    if earlier_gain_ref is not None:
        gain = gain + earlier_gain_ref[...]
    gain_out_ref[...] = gain


def wide(value):
    return value.astype(jnp.float32)


def parts_of(width):
    return [slice(first, first + CHUNK) for first in range(0, width, CHUNK)]


def halve_forward_kernel(near_ref, arrived_ref, own_ref, *send_refs):
    for part in parts_of(own_ref.shape[1]):
        total = wide(near_ref[:, part]) + wide(arrived_ref[:, part])
        own_ref[:, part] = total[:SHARD]
        for ahead, ref in enumerate(send_refs, 1):
            ref[:, part] = total[ahead * SHARD : ahead * SHARD + SHARD].astype(jnp.bfloat16)


def finish_forward_kernel(x_ref, own_ref, one_ref, two_ref, three_ref, *rest):
    out_ref = rest[-1]
    if len(rest) > 1:
        out_ref[0] = rest[0][...]
        out_ref = out_ref.at[1]
    for part in parts_of(x_ref.shape[1]):
        total = own_ref[:, part] + wide(one_ref[:, part])
        total = total + wide(two_ref[:, part]) + wide(three_ref[:, part])
        out_ref[:, part] = (wide(x_ref[:SHARD, part]) + total).astype(jnp.bfloat16)


def quarter_backward_kernel(kept_ref, one_ref, two_ref, three_ref, own_ref, send_ref):
    for part in parts_of(own_ref.shape[1]):
        total = wide(kept_ref[:, part]) + wide(one_ref[:, part])
        total = total + wide(two_ref[:, part]) + wide(three_ref[:, part])
        own_ref[:, part] = total[:SHARD]
        send_ref[:, part] = total[SHARD:].astype(jnp.bfloat16)


def finish_backward_kernel(own_ref, arrived_ref, x_ref, grad_ref, gain_ref, *rest):
    out_ref = rest[-1]
    if len(rest) > 1:
        out_ref[0] = rest[0][...]
        out_ref = out_ref.at[1]
    width = own_ref.shape[1]
    squares = jnp.zeros((SHARD, 1), jnp.float32)
    crosses = jnp.zeros((SHARD, 1), jnp.float32)
    scaled = []
    for part in parts_of(width):
        own = wide(x_ref[:SHARD, part])
        scaled.append((own_ref[:, part] + wide(arrived_ref[:, part])) * gain_ref[:, part])
        squares = squares + jnp.sum(own * own, axis=1, keepdims=True)
        crosses = crosses + jnp.sum(scaled[-1] * own, axis=1, keepdims=True)
    inverse = lax.rsqrt(squares * (1.0 / width) + EPSILON)
    factor = inverse * inverse * inverse * (crosses * (1.0 / width))
    for part, scaled_part in zip(parts_of(width), scaled):
        out_ref[:, part] = (
            wide(grad_ref[:SHARD, part])
            + inverse * scaled_part
            - wide(x_ref[:SHARD, part]) * factor
        ).astype(jnp.bfloat16)


def weight_gradient_kernel(
    normed_a,
    normed_b,
    grad_a_near,
    grad_a_far,
    grad_b_near,
    grad_b_far,
    att_a,
    att_b,
    qg_a,
    qg_b,
    kg_a,
    kg_b,
    vg_a,
    vg_b,
    gq_ref,
    gk_ref,
    gv_ref,
    go_ref,
):
    def over(top, bottom):
        return jnp.concatenate([top[...], bottom[...]], axis=0)

    part = pl.ds(pl.multiple_of(pl.program_id(0) * CHUNK, CHUNK), CHUNK)
    normed = jnp.concatenate([normed_a[:, part], normed_b[:, part]], axis=0)
    grad = jnp.concatenate(
        [ref[:, part] for ref in (grad_a_near, grad_a_far, grad_b_near, grad_b_far)], axis=0
    )
    gq_ref[...] = dot(normed, over(qg_a, qg_b), TN).astype(jnp.bfloat16)
    pair = jnp.concatenate([over(kg_a, kg_b), over(vg_a, vg_b)], axis=1)
    both = dot(normed, pair, TN).astype(jnp.bfloat16)
    gk_ref[...] = both[:, :HEAD]
    gv_ref[...] = both[:, HEAD:]
    go_ref[...] = dot(over(att_a, att_b), grad, TN).astype(jnp.bfloat16)


def estimate(flops, moved):
    return pl.CostEstimate(flops=int(flops), bytes_accessed=int(moved), transcendentals=0)


def call(kernel, out_shape, operands, flops, moved, **extra):
    return pl.pallas_call(
        kernel,
        out_shape=out_shape,
        in_specs=[extra.get("specs", {}).get(index, WHOLE) for index in range(len(operands))],
        out_specs=jax.tree.map(lambda _: WHOLE, out_shape),
        compiler_params=pltpu.CompilerParams(vmem_limit_bytes=VMEM_BYTES),
        cost_estimate=estimate(flops, moved),
        name=extra["name"],
    )(*operands)


def shaped(shape, dtype=jnp.bfloat16):
    return jax.ShapeDtypeStruct(shape, dtype)


def forward_term(pieces, gain, weights, tables):
    tokens, width = tables[0].shape[0], pieces[0].shape[1]
    size = sum(w.size for w in weights)
    return call(
        forward_kernel,
        (shaped((tokens // 2, width)), shaped((tokens // 2, width))),
        (*pieces, gain, *weights, *tables),
        4 * tokens * size,
        2 * size,
        name="layer_term",
    )


def recomputed(pieces, gain, weights, tables):
    tokens, width = tables[0].shape[0], pieces[0].shape[1]
    wq, wk, wv, _ = weights
    size = wq.size + wk.size + wv.size
    stacked = tokens * wq.shape[1] // HEAD
    return call(
        recompute_kernel,
        (
            shaped((tokens, width)),
            shaped((tokens, HEAD), jnp.float32),
            shaped((stacked, HEAD)),
            shaped((tokens, HEAD)),
            shaped((tokens, HEAD)),
            shaped((stacked, HEAD), jnp.float32),
            shaped((tokens, wq.shape[1])),
        ),
        (*pieces, gain, wq, wk, wv, *tables),
        4 * tokens * size,
        2 * size,
        name="recompute",
    )


def backward_term(grads, pieces, saved, weights, tables, *earlier_gain):
    tokens, width = tables[0].shape[0], grads[0].shape[1]
    size = sum(w.size for w in weights)
    out = call(
        backward_kernel,
        (shaped((tokens // RING, width)),) * RING
        + (
            shaped((width // CHUNK, CHUNK), jnp.float32),
            shaped((tokens, weights[0].shape[1])),
            shaped((tokens, HEAD)),
            shaped((tokens, HEAD)),
        ),
        (*grads, *pieces, *saved[1:6], *weights, *tables[:2], *earlier_gain),
        4 * tokens * size,
        2 * size,
        name="layer_gradient_term",
    )
    return out[:RING], out[RING:]


def small(kernel, out_shape, *operands):
    size = sum(x.size for x in operands)
    return call(kernel, out_shape, operands, size, 2 * size, name=kernel.__name__)


def weight_gradients(normed, grads, attended, query_grads, key_grads, value_grads):
    tokens, width = normed[0].shape
    heads = attended[0].shape[1]
    size = width * (2 * heads + 2 * HEAD)
    return pl.pallas_call(
        weight_gradient_kernel,
        grid=(width // CHUNK,),
        out_shape=(
            shaped((width, heads)),
            shaped((width, HEAD)),
            shaped((width, HEAD)),
            shaped((heads, width)),
        ),
        in_specs=[WHOLE] * 14,
        out_specs=(
            pl.BlockSpec((CHUNK, heads), lambda i: (i, 0)),
            pl.BlockSpec((CHUNK, HEAD), lambda i: (i, 0)),
            pl.BlockSpec((CHUNK, HEAD), lambda i: (i, 0)),
            pl.BlockSpec((heads, CHUNK), lambda i: (0, i)),
        ),
        compiler_params=pltpu.CompilerParams(vmem_limit_bytes=VMEM_BYTES),
        cost_estimate=estimate(4 * tokens * size, 2 * size),
        name="weight_gradients",
    )(*normed, *grads[0], *grads[1], *attended, *query_grads, *key_grads, *value_grads)


def moved(x, route, sections=None):
    count, lanes = lax.axis_size("pipe"), lax.axis_size("tensor")
    pairs = []
    for section in range(count) if sections is None else sections:
        for lane in range(lanes):
            to_section, to_lane = route(section, lane)
            if 0 <= to_section < count:
                pairs.append((section * lanes + lane, to_section * lanes + to_lane))
    return lax.ppermute(x, ("pipe", "tensor"), pairs)


def around(lane, by):
    return lane // RING * RING + (lane + by) % RING


def across(x, sections=None):
    return moved(x, lambda section, lane: (section, lane ^ RING), sections)


def from_ahead(x, sections=None):
    return [
        moved(x, lambda section, lane, by=by: (section, around(lane, -by)), sections)
        for by in range(1, RING)
    ]


def to_ahead(xs):
    return [
        moved(x, lambda section, lane, by=by: (section, around(lane, by)))
        for by, x in enumerate(xs, 1)
    ]


def forward_reduced(near, far, x, *first):
    width = near.shape[1]
    piece = shaped((SHARD, width))
    own, *sent = small(
        halve_forward_kernel,
        (shaped((SHARD, width), jnp.float32),) + (piece,) * (RING - 1),
        near,
        across(far),
    )
    out = shaped((2,) * len(first) + (SHARD, width))
    return small(finish_forward_kernel, out, x, own, *to_ahead(sent), *first)


def backward_reduced(terms, x, grad, gain, *first):
    width = terms[0].shape[1]
    own, sent = small(
        quarter_backward_kernel,
        (shaped((SHARD, width), jnp.float32), shaped((SHARD, width))),
        terms[0],
        *to_ahead(terms[1:]),
    )
    out = shaped((2,) * len(first) + (SHARD, width))
    return small(finish_backward_kernel, out, own, across(sent), x, grad, gain, *first)


def saved_pieces(rows, lane):
    blocks = [
        lax.dynamic_slice_in_dim(rows, block * SHARD, SHARD, 0) for block in (lane, lane ^ RING)
    ]
    mine = moved(
        jnp.concatenate(blocks),
        lambda section, lane: (lax.axis_size("pipe") - 1 - section, lane),
    )
    return (mine, *from_ahead(mine))


def summed_gain(gain):
    pair = gain + across(gain)
    return sum(from_ahead(pair), pair)


def per_device(
    forward_in,
    entering,
    backward_in,
    loss_grad,
    stashed,
    norm_gain,
    w_query,
    key_projection,
    value_projection,
    w_out,
):
    sections = lax.axis_size("pipe")
    section_index = lax.axis_index("pipe")
    lane = lax.axis_index("tensor")
    tables = row_tables(stashed.shape[2])
    weights = (w_query[0], key_projection[0], value_projection[0], w_out[0])
    gain = norm_gain

    own_in, own_grad = forward_in[0], backward_in[0]
    in_pair = jnp.concatenate([own_in, across(own_in)])
    in_pieces = (in_pair, *from_ahead(in_pair))
    grad_near = jnp.concatenate([own_grad, *from_ahead(own_grad)])
    first_grads = (grad_near, across(grad_near))
    pieces = [saved_pieces(stashed[0, tick], lane) for tick in range(2)]
    enter_pair = jnp.concatenate([entering, across(entering, [0])])
    last = sections - 1
    loss_near = jnp.concatenate([loss_grad, *from_ahead(loss_grad, [last])])

    first_terms = forward_term(in_pieces, gain, weights, tables)
    saved = [recomputed(rows, gain, weights, tables) for rows in pieces]
    first_back_terms, first_grad_parts = backward_term(
        first_grads, pieces[0], saved[0], weights, tables
    )
    first_out = forward_reduced(*first_terms, own_in)
    next_in = jnp.concatenate(
        [
            moved(first_out, lambda section, lane: (section + 1, lane)),
            moved(first_out, lambda section, lane: (section + 1, lane ^ RING)),
        ]
    )
    next_pair = jnp.where(section_index == 0, enter_pair, next_in)
    next_pieces = (next_pair, *from_ahead(next_pair))

    first_back = backward_reduced(first_back_terms, pieces[0][0], own_grad, gain)
    next_grad = jnp.concatenate(
        [
            moved(first_back, lambda section, lane, by=by: (section - 1, around(lane, -by)))
            for by in range(RING)
        ]
    )
    next_near = jnp.where(section_index == last, loss_near, next_grad)
    second_grads = (next_near, across(next_near))

    second_terms = forward_term(next_pieces, gain, weights, tables)
    second_back_terms, second_grad_parts = backward_term(
        second_grads, pieces[1], saved[1], weights, tables, first_grad_parts[0]
    )
    forward_out = forward_reduced(*second_terms, next_pair, first_out)
    backward_out = backward_reduced(
        second_back_terms, pieces[1][0], next_near, gain, first_back
    )
    grad_gain = summed_gain(second_grad_parts[0])
    grad_query, key_weight_gradient, value_weight_gradient, grad_out = weight_gradients(
        (saved[0][0], saved[1][0]),
        (first_grads, second_grads),
        (saved[0][6], saved[1][6]),
        (first_grad_parts[1], second_grad_parts[1]),
        (first_grad_parts[2], second_grad_parts[2]),
        (first_grad_parts[3], second_grad_parts[3]),
    )
    return (
        forward_out[:, None],
        backward_out[:, None],
        grad_query[None],
        key_weight_gradient[None],
        value_weight_gradient[None],
        grad_out[None],
        grad_gain.reshape(1, -1),
    )


def solution(mesh):
    in_specs = (
        P("pipe", "tensor", None),
        P("tensor", None),
        P("pipe", "tensor", None),
        P("tensor", None),
        P("pipe", None, None, None),
        P("pipe", None),
        P("pipe", None, "tensor"),
        P("pipe", None, "tensor"),
        P("pipe", None, "tensor"),
        P("pipe", "tensor", None),
    )
    out_specs = (
        P(None, "pipe", "tensor", None),
        P(None, "pipe", "tensor", None),
        P("pipe", None, "tensor"),
        P("pipe", None, "tensor"),
        P("pipe", None, "tensor"),
        P("pipe", "tensor", None),
        P("pipe", None),
    )
    return jax.shard_map(
        per_device, mesh=mesh, in_specs=in_specs, out_specs=out_specs, check_vma=False
    )
```

```python
import functools

import jax
import jax.numpy as jnp
import numpy as np
from jax import lax
from jax.experimental import pallas as pl
from jax.experimental.pallas import tpu as pltpu
from jax.sharding import PartitionSpec as P

HEAD = 128
EPSILON = 1e-05
ROPE_BASE = 10000.0
CHUNK = 512
LAYER_BYTES = 18 * 1024 * 1024
GRADIENT_BYTES = 14 * 1024 * 1024
SMALL_BYTES = 5 * 1024 * 1024
SETUP_BYTES = 56 * 1024 * 1024
SHARD = 16
RING = 4
WHOLE = pl.BlockSpec(memory_space=pltpu.VMEM)
SCALAR = pl.BlockSpec(memory_space=pltpu.SMEM)
AWAY = pl.BlockSpec(memory_space=pltpu.HBM)
ANYWHERE = pl.BlockSpec(memory_space=pl.ANY)

NN = (((1,), (0,)), ((), ()))
NT = (((1,), (1,)), ((), ()))
TN = (((0,), (0,)), ((), ()))


def dot(left, right, dims):
    return lax.dot_general(left, right, dims, preferred_element_type=jnp.float32)


def rope_tables(token_count):
    positions = np.arange(token_count, dtype=np.float32)[:, None]
    exponents = np.arange(HEAD // 2, dtype=np.float32) * np.float32(2.0 / HEAD)
    angles = positions * (np.float32(ROPE_BASE) ** (-exponents))[None, :]
    cosine, sine = np.cos(angles), np.sin(angles)
    return jnp.asarray(np.concatenate([cosine, cosine, -sine, sine], axis=1), jnp.float32)


def rotated(values, cosine, signed_sine):
    return values * cosine + pltpu.roll(values, HEAD // 2, 1) * signed_sine


def rotated_back(values, cosine, signed_sine):
    return values * cosine - pltpu.roll(values, HEAD // 2, 1) * signed_sine


def stacked_heads(wide):
    return jnp.concatenate(
        [wide[:, first : first + HEAD] for first in range(0, wide.shape[1], HEAD)], axis=0
    )


def side_by_side(stacked, tokens):
    return jnp.concatenate(
        [stacked[first : first + tokens] for first in range(0, stacked.shape[0], tokens)], axis=1
    )


def columns(refs, part):
    if len(refs) == 1:
        return refs[0][:, part]
    if len(refs) == 2:
        return jnp.concatenate([ref[:, part] for ref in refs], axis=0)
    pieces = [
        ref[first : first + SHARD, part] for first in (0, SHARD) for ref in refs
    ]
    return jnp.concatenate(pieces, axis=0)


def dynamic_rows(index):
    return pl.ds(pl.multiple_of(index * SHARD, SHARD), SHARD)


def attend(x_ref, gain_ref, wq_ref, wk_ref, wv_ref, tables, normed_ref=None):
    cos_ref, sin_ref, mask_ref = tables
    tokens, width = cos_ref.shape[0], wq_ref.shape[0]
    squares = jnp.zeros((tokens, HEAD), jnp.float32)
    for first in range(0, width, HEAD):
        block = columns(x_ref, slice(first, first + HEAD)).astype(jnp.float32)
        squares = squares + block * block
    inverse = lax.rsqrt(jnp.sum(squares, axis=1, keepdims=True) * (1.0 / width) + EPSILON)
    queries = jnp.zeros((tokens, wq_ref.shape[1]), jnp.float32)
    pair = jnp.zeros((tokens, 2 * HEAD), jnp.float32)
    for first in range(0, width, CHUNK):
        part = slice(first, first + CHUNK)
        normed = (
            columns(x_ref, part).astype(jnp.float32) * inverse * gain_ref[:, part]
        ).astype(jnp.bfloat16)
        if normed_ref is not None:
            normed_ref[:, part] = normed
        queries = queries + dot(normed, wq_ref[part, :], NN)
        both = jnp.concatenate([wk_ref[part, :], wv_ref[part, :]], axis=1)
        pair = pair + dot(normed, both, NN)
    cosine, sine = cos_ref[...], sin_ref[...]
    query = jnp.concatenate(
        [
            rotated(queries[:, first : first + HEAD], cosine, sine).astype(jnp.bfloat16)
            for first in range(0, queries.shape[1], HEAD)
        ],
        axis=0,
    )
    key = rotated(pair[:, :HEAD], cosine, sine).astype(jnp.bfloat16)
    value = pair[:, HEAD:].astype(jnp.bfloat16)
    scores = dot(query, key, NT) * HEAD ** (-0.5)
    causal = jnp.concatenate([mask_ref[...]] * (scores.shape[0] // tokens), axis=0) > 0.0
    terms = jnp.where(causal, jnp.exp(scores), 0.0)
    probability = terms / jnp.sum(terms, axis=1, keepdims=True)
    attended = dot(probability.astype(jnp.bfloat16), value, NN).astype(jnp.bfloat16)
    return inverse, query, key, value, probability, side_by_side(attended, tokens)


def forward_kernel(*refs):
    x_refs, (gain_ref, *projections, wo) = refs[:RING], refs[RING : RING + 5]
    tables, refs = refs[RING + 5 : RING + 8], refs[RING + 8 :]
    near_ref, far_ref = refs[-2:]
    half = near_ref.shape[0]
    attended = attend(x_refs, gain_ref, *projections, tables)[5]
    for first in range(0, wo.shape[1], CHUNK):
        part = slice(first, first + CHUNK)
        term = dot(attended, wo[:, part], NN).astype(jnp.bfloat16)
        near_ref[:, part] = term[:half]
        far_ref[:, part] = term[half:]


def recompute_kernel(first_row, *refs):
    saved_refs, (gain_ref, *projections), tables = refs[:RING], refs[RING : RING + 4], refs[8:11]
    outs = refs[-8:]
    x_ref, normed_ref, inverse_ref, query_ref, key_ref = outs[:5]
    value_ref, probability_ref, attended_ref = outs[5:]
    for flip in range(2):
        for ahead, ref in enumerate(saved_refs):
            first = (flip * RING + ahead) * SHARD
            source = flip * SHARD + (first_row if ahead else 0)
            x_ref[first : first + SHARD] = ref[source : source + SHARD, :]
    inverse, query, key, value, probability, attended = attend(
        (x_ref,), gain_ref, *projections, tables, normed_ref
    )
    inverse_ref[...] = jnp.broadcast_to(inverse, inverse_ref.shape)
    query_ref[...] = query
    key_ref[...] = key
    value_ref[...] = value
    probability_ref[...] = probability
    attended_ref[...] = attended


def backward_kernel(*refs):
    grad_refs, x_refs, refs = refs[:2], refs[2:3], refs[3:]
    inverse_ref, query_ref, key_ref, value_ref, probability_ref = refs[:5]
    (wq, wk, wv, wo), (cos_ref, sin_ref), rest = refs[5:9], refs[9:11], refs[11:]
    term_refs, rest = rest[-4 - RING : -4], rest[: -4 - RING] + rest[-4:]
    gain_out_ref, query_grad_ref, key_grad_ref, value_grad_ref = rest[-4:]
    earlier_gain_ref = rest[0] if len(rest) > 4 else None
    tokens, width = cos_ref.shape[0], wq.shape[0]
    grad_attended = jnp.zeros((tokens, wo.shape[0]), jnp.float32)
    for first in range(0, width, CHUNK):
        part = slice(first, first + CHUNK)
        grad_attended = grad_attended + dot(columns(grad_refs, part), wo[:, part], NT)
    grads = stacked_heads(grad_attended.astype(jnp.bfloat16))
    probability = probability_ref[...]
    key, value, query = key_ref[...], value_ref[...], query_ref[...]
    grad_probability = dot(grads, value, NT)
    row_terms = jnp.sum(grad_probability * probability, axis=1, keepdims=True)
    grad_scores = (
        probability * (grad_probability - row_terms) * HEAD ** (-0.5)
    ).astype(jnp.bfloat16)
    cosine, sine = cos_ref[...], sin_ref[...]
    raw = dot(grad_scores, key, NN)
    query_grad = jnp.concatenate(
        [
            rotated_back(raw[first : first + tokens], cosine, sine).astype(jnp.bfloat16)
            for first in range(0, raw.shape[0], tokens)
        ],
        axis=1,
    )
    key_grad = rotated_back(dot(grad_scores, query, TN), cosine, sine).astype(jnp.bfloat16)
    value_grad = dot(probability.astype(jnp.bfloat16), grads, TN).astype(jnp.bfloat16)
    query_grad_ref[...] = query_grad
    key_grad_ref[...] = key_grad
    value_grad_ref[...] = value_grad
    pair_grad = jnp.concatenate([key_grad, value_grad], axis=1)
    inverse = inverse_ref[:, :1]
    gains = []
    for first in range(0, width, CHUNK):
        part = slice(first, first + CHUNK)
        both = jnp.concatenate([wk[part, :], wv[part, :]], axis=1)
        term = dot(query_grad, wq[part, :], NT) + dot(pair_grad, both, NT)
        term = term.astype(jnp.bfloat16)
        for ahead, term_ref in enumerate(term_refs):
            for flip in range(2):
                start = (flip * RING + ahead) * SHARD
                rows = slice(flip * SHARD, flip * SHARD + SHARD)
                term_ref[rows, part] = term[start : start + SHARD]
        gains.append(
            jnp.sum(
                term.astype(jnp.float32) * columns(x_refs, part).astype(jnp.float32) * inverse,
                axis=0,
                keepdims=True,
            )
        )
    gain = jnp.concatenate(gains, axis=0)
    if earlier_gain_ref is None:
        gain_out_ref[...] = gain
        return
    gain = gain + earlier_gain_ref[...]
    gain_out_ref[...] = gain
    block = two_parts(gain)
    middle = block.shape[1] // 2
    block = jnp.concatenate(
        [
            block[rows, cols]
            for rows in (slice(0, 8), slice(8, 16))
            for cols in (slice(0, middle), slice(middle, 2 * middle))
        ],
        axis=0,
    ).astype(jnp.bfloat16)
    for term_ref in term_refs[1:]:
        term_ref[:, width:] = block


def two_parts(gain):
    high = wide(gain.astype(jnp.bfloat16))
    return jnp.concatenate([high, gain - high], axis=0)


def wide(value):
    return value.astype(jnp.float32)


def parts_of(width):
    return [slice(first, first + CHUNK) for first in range(0, width, CHUNK)]


def halved(near_ref, arrived_ref, own_ref, send_refs):
    for part in parts_of(own_ref.shape[1]):
        total = wide(near_ref[:, part]) + wide(arrived_ref[:, part])
        own_ref[:, part] = total[:SHARD]
        for ahead, ref in enumerate(send_refs, 1):
            ref[:SHARD, part] = total[ahead * SHARD : ahead * SHARD + SHARD].astype(jnp.bfloat16)


def halve_first_kernel(near_ref, arrived_ref, rider_ref, own_ref, *send_refs):
    halved(near_ref, arrived_ref, own_ref, send_refs)
    for ref in send_refs:
        ref[SHARD:] = rider_ref[...]


def halve_last_kernel(near_ref, arrived_ref, _, own_ref, *send_refs):
    halved(near_ref, arrived_ref, own_ref, send_refs)


def hand_on(section, edge, edge_ref, send_ref, out_ref):
    @pl.when(section == edge)
    def _():
        send_ref[...] = edge_ref[...]

    @pl.when(section != edge)
    def _():
        send_ref[...] = out_ref[...]


def finish_forward_kernel(x_ref, own_ref, one_ref, two_ref, three_ref, *rest):
    if len(rest) > 2:
        out_ref = rest[2]
    else:
        out_ref = rest[1].at[1]
        rest[1][0] = rest[0][...]
    for part in parts_of(x_ref.shape[1]):
        total = own_ref[:, part] + wide(one_ref[:SHARD, part])
        total = total + wide(two_ref[:SHARD, part]) + wide(three_ref[:SHARD, part])
        out_ref[:, part] = (wide(x_ref[:SHARD, part]) + total).astype(jnp.bfloat16)
    if len(rest) > 2:
        hand_on(rest[0][1], rest[0][2], rest[1], rest[3], out_ref)


def quartered(kept_ref, ring_refs, own_ref, send_ref):
    width = own_ref.shape[1]
    for part in parts_of(width):
        total = wide(kept_ref[:, part])
        for ref in ring_refs:
            total = total + wide(ref[:, part])
        own_ref[:, part] = total[:SHARD]
        send_ref[:, part] = total[SHARD:].astype(jnp.bfloat16)


def quarter_first_kernel(kept_ref, one_ref, two_ref, three_ref, own_ref, send_ref):
    quartered(kept_ref, (one_ref, two_ref, three_ref), own_ref, send_ref)


def quarter_last_kernel(kept_ref, one_ref, two_ref, three_ref, gain_ref, *rest):
    own_ref, send_ref, gain_out_ref = rest[-3:]
    ring_refs = (one_ref, two_ref, three_ref)
    quartered(kept_ref, ring_refs, own_ref, send_ref)
    width = own_ref.shape[1]
    gain = gain_ref[...]
    for ref in ring_refs:
        tail = wide(ref[:, width:])
        tail = tail[:SHARD] + tail[SHARD:]
        gain = gain + jnp.concatenate([tail[:8], tail[8:]], axis=1)
    gain_out_ref[...] = gain
    send_ref[:, width:] = two_parts(gain).astype(jnp.bfloat16)


def input_gradient(own_ref, arrived_ref, x_ref, grad_ref, gain_ref, out_ref):
    width = own_ref.shape[1]
    squares = jnp.zeros((SHARD, 1), jnp.float32)
    crosses = jnp.zeros((SHARD, 1), jnp.float32)
    scaled = []
    for part in parts_of(width):
        own = wide(x_ref[:SHARD, part])
        scaled.append((own_ref[:, part] + wide(arrived_ref[:, part])) * gain_ref[:, part])
        squares = squares + jnp.sum(own * own, axis=1, keepdims=True)
        crosses = crosses + jnp.sum(scaled[-1] * own, axis=1, keepdims=True)
    inverse = lax.rsqrt(squares * (1.0 / width) + EPSILON)
    factor = inverse * inverse * inverse * (crosses * (1.0 / width))
    for part, scaled_part in zip(parts_of(width), scaled):
        out_ref[:, part] = (
            wide(grad_ref[:SHARD, part])
            + inverse * scaled_part
            - wide(x_ref[:SHARD, part]) * factor
        ).astype(jnp.bfloat16)


def finish_backward_kernel(*refs):
    refs, (place_ref, edge_ref, out_ref, send_ref) = refs[:5], refs[5:]
    input_gradient(*refs, out_ref)
    hand_on(place_ref[1], 0, edge_ref, send_ref, out_ref)


def finish_last_backward_kernel(*refs):
    refs, (gain_ref, first_ref, out_ref, gain_out_ref) = refs[:5], refs[5:]
    out_ref[0] = first_ref[...]
    input_gradient(*refs, out_ref.at[1])
    width = refs[0].shape[1]
    tail = wide(refs[1][:, width:])
    gain = gain_ref[...] + tail[:8] + tail[8:]
    for index, part in enumerate(parts_of(width)):
        gain_out_ref[:, part] = gain[index : index + 1]


def join_kernel(sizes, *refs):
    outs = refs[len(refs) - len(sizes) :]
    taken = 0
    for size, out in zip(sizes, outs):
        first = 0
        for ref in refs[taken : taken + size]:
            out[first : first + ref.shape[0]] = ref[...]
            first += ref.shape[0]
        taken += size


def place_of(row, lane):
    block = lax.shift_right_logical(row, 4)
    pair = lax.shift_right_logical(lane, 2) ^ lax.shift_right_logical(block, 2)
    ring = (lane + block) & (RING - 1)
    return (pair * RING + ring) * SHARD + (row & (SHARD - 1))


def sent_rows_kernel(place_ref, stashed_ref, *refs):
    outs, sems = refs[:-1], refs[-1]
    copies = [
        pltpu.make_async_copy(
            stashed_ref.at[0, tick, dynamic_rows(block)],
            out.at[pl.ds(flip * SHARD, SHARD)],
            sems.at[tick, flip],
        )
        for tick, out in enumerate(outs)
        for flip, block in enumerate((place_ref[0], place_ref[0] ^ RING))
    ]
    for copy in copies:
        copy.start()
    for copy in copies:
        copy.wait()


def setup_kernel(place_ref, table_ref, cos_ref, sin_ref, mask_ref, place_out_ref):
    lane = place_ref[0]
    tokens = mask_ref.shape[0]
    for first in range(0, tokens, SHARD):
        block = pl.ds(pl.multiple_of(place_of(first, lane), SHARD), SHARD)
        cos_ref[first : first + SHARD] = table_ref[block, :HEAD]
        sin_ref[first : first + SHARD] = table_ref[block, HEAD:]
    later = place_of(lax.broadcasted_iota(jnp.int32, mask_ref.shape, 0), lane)
    earlier = place_of(lax.broadcasted_iota(jnp.int32, mask_ref.shape, 1), lane)
    mask_ref[...] = jnp.where(later >= earlier, 1.0, 0.0)
    for index in range(place_ref.shape[0]):
        place_out_ref[index] = place_ref[index]


def ready_kernel(*refs):
    refs[-1][...] = refs[0][...]


def stacked(refs, part=slice(None)):
    return jnp.concatenate([ref[:, part] for ref in refs], axis=0)


def this_chunk():
    return pl.ds(pl.multiple_of(pl.program_id(0) * CHUNK, CHUNK), CHUNK)


def projection_gradient_kernel(*refs):
    normed = stacked(refs[:2], this_chunk())
    gq_ref, gk_ref, gv_ref = refs[-3:]
    gq_ref[...] = dot(normed, stacked(refs[2:4]), TN).astype(jnp.bfloat16)
    pair = jnp.concatenate([stacked(refs[4:6]), stacked(refs[6:8])], axis=1)
    both = dot(normed, pair, TN).astype(jnp.bfloat16)
    gk_ref[...] = both[:, :HEAD]
    gv_ref[...] = both[:, HEAD:]


def output_gradient_kernel(*refs):
    part = this_chunk()
    refs[-1][...] = dot(stacked(refs[4:6]), stacked(refs[:4], part), TN).astype(jnp.bfloat16)


def estimate(flops, moved):
    return pl.CostEstimate(flops=int(flops), bytes_accessed=int(moved), transcendentals=0)


def call(
    kernel, out_shape, operands, flops, moved, name, room, specs=None, scratch=(), last_scalar=False
):
    out_specs = jax.tree.map(lambda _: WHOLE, out_shape)
    if last_scalar:
        out_specs = out_specs[:-1] + (SCALAR,)
    return pl.pallas_call(
        kernel,
        out_shape=out_shape,
        in_specs=[(specs or {}).get(index, WHOLE) for index in range(len(operands))],
        out_specs=out_specs,
        scratch_shapes=list(scratch),
        compiler_params=pltpu.CompilerParams(vmem_limit_bytes=room),
        cost_estimate=estimate(flops, moved),
        name=name,
    )(*operands)


def shaped(shape, dtype=jnp.bfloat16):
    return jax.ShapeDtypeStruct(shape, dtype)


def layer_call(kernel, out_shape, before, weights, after, name, specs=None):
    tokens, size = 8 * SHARD, sum(w.size for w in weights)
    operands = (*before, *weights, *after)
    return call(kernel, out_shape, operands, 4 * tokens * size, 2 * size, name, LAYER_BYTES, specs)


def forward_term(pieces, gain, weights, tables, *after):
    half = shaped((tables[0].shape[0] // 2, pieces[0].shape[1]))
    count = len(pieces) + 1 + len(weights) + len(tables)
    return layer_call(
        forward_kernel,
        (half, half),
        (*pieces, gain),
        weights,
        (*tables, *after),
        "layer_term",
        {count + index: ANYWHERE for index in range(len(after))},
    )


def recomputed(pieces, first_row, gain, weights, tables):
    tokens, width = tables[0].shape[0], pieces[0].shape[1]
    heads = weights[0].shape[1]
    stacked_rows = tokens * heads // HEAD
    return layer_call(
        functools.partial(recompute_kernel, first_row),
        (
            shaped((tokens, width)),
            shaped((tokens, width)),
            shaped((tokens, HEAD), jnp.float32),
            shaped((stacked_rows, HEAD)),
            shaped((tokens, HEAD)),
            shaped((tokens, HEAD)),
            shaped((stacked_rows, HEAD), jnp.float32),
            shaped((tokens, heads)),
        ),
        (*pieces, gain),
        weights[:3],
        tables,
        "recompute",
    )


def backward_term(grads, saved, weights, tables, *earlier_gain):
    tokens, width = tables[0].shape[0], grads[0].shape[1]
    extra = 2 * width // (tokens // RING) if earlier_gain else 0
    out = layer_call(
        backward_kernel,
        (shaped((tokens // RING, width)),)
        + (shaped((tokens // RING, width + extra)),) * (RING - 1)
        + (
            shaped((width // CHUNK, CHUNK), jnp.float32),
            shaped((tokens, weights[0].shape[1])),
            shaped((tokens, HEAD)),
            shaped((tokens, HEAD)),
        ),
        (*grads, saved[0], *saved[2:7]),
        weights,
        (*tables[:2], *earlier_gain),
        "layer_gradient_term",
    )
    return out[:RING], out[RING:]


def small(kernel, out_shape, *operands, specs=None, scratch=()):
    size = sum(x.size for x in operands)
    return call(
        kernel, out_shape, operands, size, 2 * size, kernel.__name__, SMALL_BYTES, specs, scratch
    )


def joined(groups, *after):
    operands = [x for group in groups for x in group]
    outs = tuple(
        shaped((sum(x.shape[0] for x in group), group[0].shape[1])) for group in groups
    )
    size = sum(x.size for x in operands)
    return call(
        functools.partial(join_kernel, [len(group) for group in groups]),
        outs,
        (*operands, *after),
        size,
        2 * size,
        "joined",
        SMALL_BYTES,
        specs={len(operands) + index: ANYWHERE for index in range(len(after))},
    )


def weight_gradient(kernel, operands, out_shape, out_specs, after):
    chunks = max(out_shape[0].shape) // CHUNK
    size = sum(x.size for x in out_shape)
    return pl.pallas_call(
        kernel,
        grid=(chunks,),
        out_shape=out_shape,
        in_specs=[WHOLE] * len(operands) + [ANYWHERE],
        out_specs=out_specs,
        compiler_params=pltpu.CompilerParams(vmem_limit_bytes=GRADIENT_BYTES),
        cost_estimate=estimate(4 * 8 * SHARD * size, 2 * size),
        name=kernel.__name__,
    )(*operands, after)


def projection_gradients(normed, query_grads, key_grads, value_grads, after):
    width, heads = normed[0].shape[1], query_grads[0].shape[1]
    return weight_gradient(
        projection_gradient_kernel,
        (*normed, *query_grads, *key_grads, *value_grads),
        tuple(shaped((width, columns)) for columns in (heads, HEAD, HEAD)),
        tuple(pl.BlockSpec((CHUNK, columns), lambda i: (i, 0)) for columns in (heads, HEAD, HEAD)),
        after,
    )


def output_gradient(grads, attended, after):
    heads, width = attended[0].shape[1], grads[0].shape[1]
    return weight_gradient(
        output_gradient_kernel,
        (*grads, *attended),
        (shaped((heads, width)),),
        (pl.BlockSpec((heads, CHUNK), lambda i: (0, i)),),
        after,
    )[0]


def moved(x, route):
    count, lanes = lax.axis_size("pipe"), lax.axis_size("tensor")
    pairs = []
    for section in range(count):
        for lane in range(lanes):
            to_section, to_lane = route(section, lane)
            pairs.append((section * lanes + lane, to_section % count * lanes + to_lane))
    return lax.ppermute(x, ("pipe", "tensor"), pairs)


def around(lane, by):
    return lane // RING * RING + (lane + by) % RING


def across(x):
    return moved(x, lambda section, lane: (section, lane ^ RING))


def from_ahead(x):
    return [
        moved(x, lambda section, lane, by=by: (section, around(lane, -by)))
        for by in range(1, RING)
    ]


def to_ahead(xs):
    return [
        moved(x, lambda section, lane, by=by: (section, around(lane, by)))
        for by, x in enumerate(xs, 1)
    ]


def halve_shapes(near, riders):
    width = near.shape[1]
    piece = shaped((SHARD + riders, width))
    return (shaped((SHARD, width), jnp.float32),) + (piece,) * (RING - 1)


def quarter_shapes(terms):
    width, extra = terms[0].shape[1], terms[1].shape[1] - terms[0].shape[1]
    return shaped((SHARD, width), jnp.float32), shaped((SHARD, width + 2 * extra))


def sent_rows(place, stashed):
    _, _, _, width = stashed.shape
    return call(
        sent_rows_kernel,
        (shaped((2 * SHARD, width)),) * 2,
        (place, stashed),
        0,
        8 * SHARD * width,
        "sent_rows",
        SETUP_BYTES,
        specs={0: SCALAR, 1: AWAY},
        scratch=[pltpu.SemaphoreType.DMA((2, 2))],
    )


def set_up(place, tokens):
    table = shaped((tokens, HEAD), jnp.float32)
    out = call(
        setup_kernel,
        (table, table, shaped((tokens, tokens), jnp.float32), shaped(place.shape, jnp.int32)),
        (place, rope_tables(tokens)),
        tokens * HEAD,
        4 * tokens * HEAD,
        "setup",
        SMALL_BYTES,
        specs={0: SCALAR},
        last_scalar=True,
    )
    return out[:3], out[3]


def made_ready(table, weights):
    size = sum(w.size for w in weights)
    return call(
        ready_kernel, shaped(table.shape, jnp.float32), (table, *weights), 0, 2 * size,
        "weights_ready", LAYER_BYTES,
    )


def mirrored(rows):
    return moved(rows, lambda section, lane: (-1 - section, lane))


def per_device(
    forward_in,
    entering,
    backward_in,
    loss_grad,
    stashed,
    norm_gain,
    w_query,
    key_projection,
    value_projection,
    w_out,
):
    place = jnp.stack(
        [lax.axis_index("tensor"), lax.axis_index("pipe"), lax.axis_size("pipe") - 1]
    ).astype(jnp.int32)
    sent_pairs = sent_rows(place, stashed)
    tables, place = set_up(place, stashed.shape[2])
    weights = (w_query[0], key_projection[0], value_projection[0], w_out[0])
    tables = (made_ready(tables[0], weights), *tables[1:])
    gain = norm_gain
    own_in, own_grad = forward_in[0], backward_in[0]
    row = shaped(own_in.shape)
    both = shaped((2,) + row.shape)

    first_pair, second_pair = [mirrored(pair) for pair in sent_pairs]
    (in_pair,) = joined([(own_in, across(own_in))])
    in_pieces = (in_pair, *from_ahead(in_pair))
    grad_near, entering, loss_grad = joined(
        [(own_grad, *from_ahead(own_grad)), (entering,), (loss_grad,)], tables[0]
    )
    first_grads = (grad_near, across(grad_near))
    first_rows = (first_pair, *from_ahead(first_pair))
    first_terms = forward_term(in_pieces, gain, weights, tables)
    first_states = recomputed(first_rows, 0, gain, weights, tables)
    first_back_terms, first_grad_parts = backward_term(
        first_grads, first_states, weights, tables
    )
    own, *sent = small(
        halve_first_kernel, halve_shapes(first_terms[0], 2 * SHARD), first_terms[0],
        across(first_terms[1]), second_pair,
    )
    arrived = to_ahead(sent)
    second_rows = (second_pair, *arrived[::-1])
    first_out, handed_out = small(
        finish_forward_kernel, (row, row), in_pair, own, *arrived, place, entering,
        specs={5: SCALAR},
    )
    own, sent = small(
        quarter_first_kernel, quarter_shapes(first_back_terms),
        first_back_terms[0], *to_ahead(first_back_terms[1:]),
    )
    first_back, handed_back = small(
        finish_backward_kernel, (row, row), own, across(sent), first_states[0], grad_near, gain,
        place, loss_grad, specs={5: SCALAR},
    )

    next_pair, next_near = joined(
        [
            (
                moved(handed_out, lambda section, lane: (section + 1, lane)),
                moved(handed_out, lambda section, lane: (section + 1, lane ^ RING)),
            ),
            [
                moved(handed_back, lambda section, lane, by=by: (section - 1, around(lane, -by)))
                for by in range(RING)
            ],
        ]
    )
    next_pieces = (next_pair, *from_ahead(next_pair))
    second_grads = (next_near, across(next_near))
    second_states = recomputed(second_rows, SHARD, gain, weights, tables)
    second_terms = forward_term(next_pieces, gain, weights, tables, second_grads[1])
    second_back_terms, second_grad_parts = backward_term(
        second_grads, second_states, weights, tables, first_grad_parts[0]
    )
    grad_out = output_gradient(
        (*first_grads, *second_grads), (first_states[7], second_states[7]), second_grad_parts[0]
    )
    forward_own, *sent = small(
        halve_last_kernel, halve_shapes(second_terms[0], 0), second_terms[0],
        across(second_terms[1]), grad_out, specs={2: ANYWHERE},
    )
    arrived = to_ahead(sent)
    forward_out = small(
        finish_forward_kernel, both, next_pair, forward_own, *arrived, first_out
    )
    own, sent, gain_sum = small(
        quarter_last_kernel,
        (*quarter_shapes(second_back_terms), shaped(second_grad_parts[0].shape, jnp.float32)),
        second_back_terms[0], *to_ahead(second_back_terms[1:]), second_grad_parts[0],
        arrived[0], specs={RING + 1: ANYWHERE},
    )
    grad_query, key_weight_gradient, value_weight_gradient = projection_gradients(
        (first_states[1], second_states[1]),
        *[(first_grad_parts[index], second_grad_parts[index]) for index in (1, 2, 3)],
        own,
    )
    backward_out, grad_gain = small(
        finish_last_backward_kernel,
        (both, shaped(gain.shape, jnp.float32)),
        own, across(sent), second_states[0], next_near, gain, gain_sum, first_back,
    )
    return (
        forward_out[:, None],
        backward_out[:, None],
        grad_query[None],
        key_weight_gradient[None],
        value_weight_gradient[None],
        grad_out[None],
        grad_gain,
    )


def solution(mesh):
    in_specs = (
        P("pipe", "tensor", None),
        P("tensor", None),
        P("pipe", "tensor", None),
        P("tensor", None),
        P("pipe", None, None, None),
        P("pipe", None),
        P("pipe", None, "tensor"),
        P("pipe", None, "tensor"),
        P("pipe", None, "tensor"),
        P("pipe", "tensor", None),
    )
    out_specs = (
        P(None, "pipe", "tensor", None),
        P(None, "pipe", "tensor", None),
        P("pipe", None, "tensor"),
        P("pipe", None, "tensor"),
        P("pipe", None, "tensor"),
        P("pipe", "tensor", None),
        P("pipe", None),
    )
    return jax.shard_map(
        per_device, mesh=mesh, in_specs=in_specs, out_specs=out_specs, check_vma=False
    )
```

```python
import functools

import jax
import jax.numpy as jnp
import numpy as np
from jax import lax
from jax.experimental import pallas as pl
from jax.experimental.pallas import tpu as pltpu
from jax.sharding import PartitionSpec as P

HEAD = 128
EPSILON = 1e-05
ROPE_BASE = 10000.0
CHUNK = 512
LAYER_BYTES = 18 * 1024 * 1024
GRADIENT_BYTES = 14 * 1024 * 1024
SMALL_BYTES = 5 * 1024 * 1024
SETUP_BYTES = 56 * 1024 * 1024
SHARD = 16
RING = 4
WHOLE = pl.BlockSpec(memory_space=pltpu.VMEM)
SCALAR = pl.BlockSpec(memory_space=pltpu.SMEM)
AWAY = pl.BlockSpec(memory_space=pltpu.HBM)
ANYWHERE = pl.BlockSpec(memory_space=pl.ANY)

NN = (((1,), (0,)), ((), ()))
NT = (((1,), (1,)), ((), ()))
TN = (((0,), (0,)), ((), ()))


def dot(left, right, dims):
    return lax.dot_general(left, right, dims, preferred_element_type=jnp.float32)


def rope_tables(token_count):
    positions = np.arange(token_count, dtype=np.float32)[:, None]
    exponents = np.arange(HEAD // 2, dtype=np.float32) * np.float32(2.0 / HEAD)
    angles = positions * (np.float32(ROPE_BASE) ** (-exponents))[None, :]
    cosine, sine = np.cos(angles), np.sin(angles)
    return jnp.asarray(np.concatenate([cosine, cosine, -sine, sine], axis=1), jnp.float32)


def rotated(values, cosine, signed_sine):
    return values * cosine + pltpu.roll(values, HEAD // 2, 1) * signed_sine


def rotated_back(values, cosine, signed_sine):
    return values * cosine - pltpu.roll(values, HEAD // 2, 1) * signed_sine


def stacked_heads(wide):
    return jnp.concatenate(
        [wide[:, first : first + HEAD] for first in range(0, wide.shape[1], HEAD)], axis=0
    )


def side_by_side(stacked, tokens):
    return jnp.concatenate(
        [stacked[first : first + tokens] for first in range(0, stacked.shape[0], tokens)], axis=1
    )


def columns(refs, part):
    if len(refs) == 1:
        return refs[0][:, part]
    if len(refs) == 2:
        return jnp.concatenate([ref[:, part] for ref in refs], axis=0)
    pieces = [
        ref[first : first + SHARD, part] for first in (0, SHARD) for ref in refs
    ]
    return jnp.concatenate(pieces, axis=0)


def dynamic_rows(index):
    return pl.ds(pl.multiple_of(index * SHARD, SHARD), SHARD)


def attend(x_ref, gain_ref, wq_ref, wk_ref, wv_ref, tables, normed_ref=None):
    cos_ref, sin_ref, mask_ref = tables
    tokens, width = cos_ref.shape[0], wq_ref.shape[0]
    squares = jnp.zeros((tokens, HEAD), jnp.float32)
    for first in range(0, width, HEAD):
        block = columns(x_ref, slice(first, first + HEAD)).astype(jnp.float32)
        squares = squares + block * block
    inverse = lax.rsqrt(jnp.sum(squares, axis=1, keepdims=True) * (1.0 / width) + EPSILON)
    queries = jnp.zeros((tokens, wq_ref.shape[1]), jnp.float32)
    pair = jnp.zeros((tokens, 2 * HEAD), jnp.float32)
    for first in range(0, width, CHUNK):
        part = slice(first, first + CHUNK)
        normed = (
            columns(x_ref, part).astype(jnp.float32) * inverse * gain_ref[:, part]
        ).astype(jnp.bfloat16)
        if normed_ref is not None:
            normed_ref[:, part] = normed
        queries = queries + dot(normed, wq_ref[part, :], NN)
        both = jnp.concatenate([wk_ref[part, :], wv_ref[part, :]], axis=1)
        pair = pair + dot(normed, both, NN)
    cosine, sine = cos_ref[...], sin_ref[...]
    query = jnp.concatenate(
        [
            rotated(queries[:, first : first + HEAD], cosine, sine).astype(jnp.bfloat16)
            for first in range(0, queries.shape[1], HEAD)
        ],
        axis=0,
    )
    key = rotated(pair[:, :HEAD], cosine, sine).astype(jnp.bfloat16)
    value = pair[:, HEAD:].astype(jnp.bfloat16)
    scores = dot(query, key, NT) * HEAD ** (-0.5)
    causal = jnp.concatenate([mask_ref[...]] * (scores.shape[0] // tokens), axis=0) > 0.0
    terms = jnp.where(causal, jnp.exp(scores), 0.0)
    probability = terms / jnp.sum(terms, axis=1, keepdims=True)
    attended = dot(probability.astype(jnp.bfloat16), value, NN).astype(jnp.bfloat16)
    return inverse, query, key, value, probability, side_by_side(attended, tokens)


def forward_kernel(*refs):
    x_refs, (gain_ref, *projections, wo) = refs[:RING], refs[RING : RING + 5]
    tables, refs = refs[RING + 5 : RING + 8], refs[RING + 8 :]
    near_ref, far_ref = refs[-2:]
    half = near_ref.shape[0]
    attended = attend(x_refs, gain_ref, *projections, tables)[5]
    for first in range(0, wo.shape[1], CHUNK):
        part = slice(first, first + CHUNK)
        term = dot(attended, wo[:, part], NN).astype(jnp.bfloat16)
        near_ref[:, part] = term[:half]
        far_ref[:, part] = term[half:]


def recompute_kernel(first_row, *refs):
    saved_refs, (gain_ref, *projections), tables = refs[:RING], refs[RING : RING + 4], refs[8:11]
    outs = refs[-8:]
    x_ref, normed_ref, inverse_ref, query_ref, key_ref = outs[:5]
    value_ref, probability_ref, attended_ref = outs[5:]
    for flip in range(2):
        for ahead, ref in enumerate(saved_refs):
            first = (flip * RING + ahead) * SHARD
            source = flip * SHARD + (first_row if ahead else 0)
            x_ref[first : first + SHARD] = ref[source : source + SHARD, :]
    inverse, query, key, value, probability, attended = attend(
        (x_ref,), gain_ref, *projections, tables, normed_ref
    )
    inverse_ref[...] = jnp.broadcast_to(inverse, inverse_ref.shape)
    query_ref[...] = query
    key_ref[...] = key
    value_ref[...] = value
    probability_ref[...] = probability
    attended_ref[...] = attended


def backward_kernel(*refs):
    grad_refs, x_refs, refs = refs[:2], refs[2:3], refs[3:]
    inverse_ref, query_ref, key_ref, value_ref, probability_ref = refs[:5]
    (wq, wk, wv, wo), (cos_ref, sin_ref), rest = refs[5:9], refs[9:11], refs[11:]
    term_refs, rest = rest[-4 - RING : -4], rest[: -4 - RING] + rest[-4:]
    gain_out_ref, query_grad_ref, key_grad_ref, value_grad_ref = rest[-4:]
    earlier_gain_ref = rest[0] if len(rest) > 4 else None
    tokens, width = cos_ref.shape[0], wq.shape[0]
    grad_attended = jnp.zeros((tokens, wo.shape[0]), jnp.float32)
    for first in range(0, width, CHUNK):
        part = slice(first, first + CHUNK)
        grad_attended = grad_attended + dot(columns(grad_refs, part), wo[:, part], NT)
    grads = stacked_heads(grad_attended.astype(jnp.bfloat16))
    probability = probability_ref[...]
    key, value, query = key_ref[...], value_ref[...], query_ref[...]
    grad_probability = dot(grads, value, NT)
    row_terms = jnp.sum(grad_probability * probability, axis=1, keepdims=True)
    grad_scores = (
        probability * (grad_probability - row_terms) * HEAD ** (-0.5)
    ).astype(jnp.bfloat16)
    cosine, sine = cos_ref[...], sin_ref[...]
    raw = dot(grad_scores, key, NN)
    query_grad = jnp.concatenate(
        [
            rotated_back(raw[first : first + tokens], cosine, sine).astype(jnp.bfloat16)
            for first in range(0, raw.shape[0], tokens)
        ],
        axis=1,
    )
    key_grad = rotated_back(dot(grad_scores, query, TN), cosine, sine).astype(jnp.bfloat16)
    value_grad = dot(probability.astype(jnp.bfloat16), grads, TN).astype(jnp.bfloat16)
    query_grad_ref[...] = query_grad
    key_grad_ref[...] = key_grad
    value_grad_ref[...] = value_grad
    pair_grad = jnp.concatenate([key_grad, value_grad], axis=1)
    inverse = inverse_ref[:, :1]
    gains = []
    for first in range(0, width, CHUNK):
        part = slice(first, first + CHUNK)
        both = jnp.concatenate([wk[part, :], wv[part, :]], axis=1)
        term = dot(query_grad, wq[part, :], NT) + dot(pair_grad, both, NT)
        term = term.astype(jnp.bfloat16)
        for ahead, term_ref in enumerate(term_refs):
            for flip in range(2):
                start = (flip * RING + ahead) * SHARD
                rows = slice(flip * SHARD, flip * SHARD + SHARD)
                term_ref[rows, part] = term[start : start + SHARD]
        gains.append(
            jnp.sum(
                term.astype(jnp.float32) * columns(x_refs, part).astype(jnp.float32) * inverse,
                axis=0,
                keepdims=True,
            )
        )
    gain = jnp.concatenate(gains, axis=0)
    if earlier_gain_ref is None:
        gain_out_ref[...] = gain
        return
    gain = gain + earlier_gain_ref[...]
    gain_out_ref[...] = gain
    block = two_parts(gain)
    middle = block.shape[1] // 2
    block = jnp.concatenate(
        [
            block[rows, cols]
            for rows in (slice(0, 8), slice(8, 16))
            for cols in (slice(0, middle), slice(middle, 2 * middle))
        ],
        axis=0,
    ).astype(jnp.bfloat16)
    for term_ref in term_refs[1:]:
        term_ref[:, width:] = block


def two_parts(gain):
    high = wide(gain.astype(jnp.bfloat16))
    return jnp.concatenate([high, gain - high], axis=0)


def wide(value):
    return value.astype(jnp.float32)


def parts_of(width):
    return [slice(first, first + CHUNK) for first in range(0, width, CHUNK)]


def halved(near_ref, arrived_ref, own_ref, send_refs):
    for part in parts_of(own_ref.shape[1]):
        total = wide(near_ref[:, part]) + wide(arrived_ref[:, part])
        own_ref[:, part] = total[:SHARD]
        for ahead, ref in enumerate(send_refs, 1):
            ref[:SHARD, part] = total[ahead * SHARD : ahead * SHARD + SHARD].astype(jnp.bfloat16)


def halve_first_kernel(near_ref, arrived_ref, rider_ref, own_ref, *send_refs):
    halved(near_ref, arrived_ref, own_ref, send_refs)
    for ref in send_refs:
        ref[SHARD:] = rider_ref[...]


def halve_last_kernel(near_ref, arrived_ref, _, own_ref, *send_refs):
    halved(near_ref, arrived_ref, own_ref, send_refs)


def hand_on(section, edge, edge_ref, send_ref, out_ref):
    @pl.when(section == edge)
    def _():
        send_ref[...] = edge_ref[...]

    @pl.when(section != edge)
    def _():
        send_ref[...] = out_ref[...]


def finish_forward_kernel(x_ref, own_ref, one_ref, two_ref, three_ref, *rest):
    if len(rest) > 2:
        out_ref = rest[2]
    else:
        out_ref = rest[1].at[1]
        rest[1][0] = rest[0][...]
    for part in parts_of(x_ref.shape[1]):
        total = own_ref[:, part] + wide(one_ref[:SHARD, part])
        total = total + wide(two_ref[:SHARD, part]) + wide(three_ref[:SHARD, part])
        out_ref[:, part] = (wide(x_ref[:SHARD, part]) + total).astype(jnp.bfloat16)
    if len(rest) > 2:
        hand_on(rest[0][1], rest[0][2], rest[1], rest[3], out_ref)


def quartered(kept_ref, ring_refs, own_ref, send_ref):
    width = own_ref.shape[1]
    for part in parts_of(width):
        total = wide(kept_ref[:, part])
        for ref in ring_refs:
            total = total + wide(ref[:, part])
        own_ref[:, part] = total[:SHARD]
        send_ref[:, part] = total[SHARD:].astype(jnp.bfloat16)


def quarter_first_kernel(kept_ref, one_ref, two_ref, three_ref, own_ref, send_ref):
    quartered(kept_ref, (one_ref, two_ref, three_ref), own_ref, send_ref)


def quarter_last_kernel(kept_ref, one_ref, two_ref, three_ref, gain_ref, *rest):
    own_ref, send_ref, gain_out_ref = rest[-3:]
    ring_refs = (one_ref, two_ref, three_ref)
    quartered(kept_ref, ring_refs, own_ref, send_ref)
    width = own_ref.shape[1]
    gain = gain_ref[...]
    for ref in ring_refs:
        tail = wide(ref[:, width:])
        tail = tail[:SHARD] + tail[SHARD:]
        gain = gain + jnp.concatenate([tail[:8], tail[8:]], axis=1)
    gain_out_ref[...] = gain
    send_ref[:, width:] = two_parts(gain).astype(jnp.bfloat16)


def input_gradient(own_ref, arrived_ref, x_ref, grad_ref, gain_ref, out_ref):
    width = own_ref.shape[1]
    squares = jnp.zeros((SHARD, 1), jnp.float32)
    crosses = jnp.zeros((SHARD, 1), jnp.float32)
    scaled = []
    for part in parts_of(width):
        own = wide(x_ref[:SHARD, part])
        scaled.append((own_ref[:, part] + wide(arrived_ref[:, part])) * gain_ref[:, part])
        squares = squares + jnp.sum(own * own, axis=1, keepdims=True)
        crosses = crosses + jnp.sum(scaled[-1] * own, axis=1, keepdims=True)
    inverse = lax.rsqrt(squares * (1.0 / width) + EPSILON)
    factor = inverse * inverse * inverse * (crosses * (1.0 / width))
    for part, scaled_part in zip(parts_of(width), scaled):
        out_ref[:, part] = (
            wide(grad_ref[:SHARD, part])
            + inverse * scaled_part
            - wide(x_ref[:SHARD, part]) * factor
        ).astype(jnp.bfloat16)


def finish_backward_kernel(*refs):
    refs, (place_ref, edge_ref, out_ref, send_ref) = refs[:5], refs[5:]
    input_gradient(*refs, out_ref)
    hand_on(place_ref[1], 0, edge_ref, send_ref, out_ref)


def finish_last_backward_kernel(*refs):
    refs, (gain_ref, first_ref, out_ref, gain_out_ref) = refs[:5], refs[5:]
    out_ref[0] = first_ref[...]
    input_gradient(*refs, out_ref.at[1])
    width = refs[0].shape[1]
    tail = wide(refs[1][:, width:])
    gain = gain_ref[...] + tail[:8] + tail[8:]
    for index, part in enumerate(parts_of(width)):
        gain_out_ref[:, part] = gain[index : index + 1]


def join_kernel(sizes, *refs):
    outs = refs[len(refs) - len(sizes) :]
    taken = 0
    for size, out in zip(sizes, outs):
        first = 0
        for ref in refs[taken : taken + size]:
            out[first : first + ref.shape[0]] = ref[...]
            first += ref.shape[0]
        taken += size


def place_of(row, lane):
    block = lax.shift_right_logical(row, 4)
    pair = lax.shift_right_logical(lane, 2) ^ lax.shift_right_logical(block, 2)
    ring = (lane + block) & (RING - 1)
    return (pair * RING + ring) * SHARD + (row & (SHARD - 1))


def sent_rows_kernel(place_ref, stashed_ref, *refs):
    outs, sems = refs[:-1], refs[-1]
    copies = [
        pltpu.make_async_copy(
            stashed_ref.at[0, tick, dynamic_rows(block)],
            out.at[pl.ds(flip * SHARD, SHARD)],
            sems.at[tick, flip],
        )
        for tick, out in enumerate(outs)
        for flip, block in enumerate((place_ref[0], place_ref[0] ^ RING))
    ]
    for copy in copies:
        copy.start()
    for copy in copies:
        copy.wait()


def setup_kernel(place_ref, table_ref, cos_ref, sin_ref, mask_ref, place_out_ref):
    lane = place_ref[0]
    tokens = mask_ref.shape[0]
    for first in range(0, tokens, SHARD):
        block = pl.ds(pl.multiple_of(place_of(first, lane), SHARD), SHARD)
        cos_ref[first : first + SHARD] = table_ref[block, :HEAD]
        sin_ref[first : first + SHARD] = table_ref[block, HEAD:]
    later = place_of(lax.broadcasted_iota(jnp.int32, mask_ref.shape, 0), lane)
    earlier = place_of(lax.broadcasted_iota(jnp.int32, mask_ref.shape, 1), lane)
    mask_ref[...] = jnp.where(later >= earlier, 1.0, 0.0)
    for index in range(place_ref.shape[0]):
        place_out_ref[index] = place_ref[index]


def ready_kernel(*refs):
    refs[-1][...] = refs[0][...]


def stacked(refs, part=slice(None)):
    return jnp.concatenate([ref[:, part] for ref in refs], axis=0)


def this_chunk():
    return pl.ds(pl.multiple_of(pl.program_id(0) * CHUNK, CHUNK), CHUNK)


def projection_gradient_kernel(*refs):
    normed = stacked(refs[:2], this_chunk())
    gq_ref, gk_ref, gv_ref = refs[-3:]
    gq_ref[...] = dot(normed, stacked(refs[2:4]), TN).astype(jnp.bfloat16)
    pair = jnp.concatenate([stacked(refs[4:6]), stacked(refs[6:8])], axis=1)
    both = dot(normed, pair, TN).astype(jnp.bfloat16)
    gk_ref[...] = both[:, :HEAD]
    gv_ref[...] = both[:, HEAD:]


def output_gradient_kernel(*refs):
    part = this_chunk()
    refs[-2][...] = dot(stacked(refs[4:6]), stacked(refs[:4], part), TN).astype(jnp.bfloat16)
    refs[-1][...] = jnp.zeros(refs[-1].shape, jnp.float32)


def estimate(flops, moved):
    return pl.CostEstimate(flops=int(flops), bytes_accessed=int(moved), transcendentals=0)


def call(
    kernel, out_shape, operands, flops, moved, name, room, specs=None, scratch=(), last_scalar=False
):
    out_specs = jax.tree.map(lambda _: WHOLE, out_shape)
    if last_scalar:
        out_specs = out_specs[:-1] + (SCALAR,)
    return pl.pallas_call(
        kernel,
        out_shape=out_shape,
        in_specs=[(specs or {}).get(index, WHOLE) for index in range(len(operands))],
        out_specs=out_specs,
        scratch_shapes=list(scratch),
        compiler_params=pltpu.CompilerParams(vmem_limit_bytes=room),
        cost_estimate=estimate(flops, moved),
        name=name,
    )(*operands)


def shaped(shape, dtype=jnp.bfloat16):
    return jax.ShapeDtypeStruct(shape, dtype)


def layer_call(kernel, out_shape, before, weights, after, name, specs=None):
    tokens, size = 8 * SHARD, sum(w.size for w in weights)
    operands = (*before, *weights, *after)
    return call(kernel, out_shape, operands, 4 * tokens * size, 2 * size, name, LAYER_BYTES, specs)


def forward_term(pieces, gain, weights, tables, *after):
    half = shaped((tables[0].shape[0] // 2, pieces[0].shape[1]))
    count = len(pieces) + 1 + len(weights) + len(tables)
    return layer_call(
        forward_kernel,
        (half, half),
        (*pieces, gain),
        weights,
        (*tables, *after),
        "layer_term",
        {count + index: ANYWHERE for index in range(len(after))},
    )


def recomputed(pieces, first_row, gain, weights, tables):
    tokens, width = tables[0].shape[0], pieces[0].shape[1]
    heads = weights[0].shape[1]
    stacked_rows = tokens * heads // HEAD
    return layer_call(
        functools.partial(recompute_kernel, first_row),
        (
            shaped((tokens, width)),
            shaped((tokens, width)),
            shaped((tokens, HEAD), jnp.float32),
            shaped((stacked_rows, HEAD)),
            shaped((tokens, HEAD)),
            shaped((tokens, HEAD)),
            shaped((stacked_rows, HEAD), jnp.float32),
            shaped((tokens, heads)),
        ),
        (*pieces, gain),
        weights[:3],
        tables,
        "recompute",
    )


def backward_term(grads, saved, weights, tables, *earlier_gain):
    tokens, width = tables[0].shape[0], grads[0].shape[1]
    extra = 2 * width // (tokens // RING) if earlier_gain else 0
    out = layer_call(
        backward_kernel,
        (shaped((tokens // RING, width)),)
        + (shaped((tokens // RING, width + extra)),) * (RING - 1)
        + (
            shaped((width // CHUNK, CHUNK), jnp.float32),
            shaped((tokens, weights[0].shape[1])),
            shaped((tokens, HEAD)),
            shaped((tokens, HEAD)),
        ),
        (*grads, saved[0], *saved[2:7]),
        weights,
        (*tables[:2], *earlier_gain),
        "layer_gradient_term",
    )
    return out[:RING], out[RING:]


def small(kernel, out_shape, *operands, specs=None, scratch=()):
    size = sum(x.size for x in operands)
    return call(
        kernel, out_shape, operands, size, 2 * size, kernel.__name__, SMALL_BYTES, specs, scratch
    )


def joined(groups, *after):
    operands = [x for group in groups for x in group]
    outs = tuple(
        shaped((sum(x.shape[0] for x in group), group[0].shape[1])) for group in groups
    )
    size = sum(x.size for x in operands)
    return call(
        functools.partial(join_kernel, [len(group) for group in groups]),
        outs,
        (*operands, *after),
        size,
        2 * size,
        "joined",
        SMALL_BYTES,
        specs={len(operands) + index: ANYWHERE for index in range(len(after))},
    )


def weight_gradient(kernel, operands, out_shape, out_specs, after):
    chunks = max(out_shape[0].shape) // CHUNK
    size = sum(x.size for x in out_shape)
    return pl.pallas_call(
        kernel,
        grid=(chunks,),
        out_shape=out_shape,
        in_specs=[WHOLE] * len(operands) + [ANYWHERE],
        out_specs=out_specs,
        compiler_params=pltpu.CompilerParams(vmem_limit_bytes=GRADIENT_BYTES),
        cost_estimate=estimate(4 * 8 * SHARD * size, 2 * size),
        name=kernel.__name__,
    )(*operands, after)


def projection_gradients(normed, query_grads, key_grads, value_grads, after):
    width, heads = normed[0].shape[1], query_grads[0].shape[1]
    return weight_gradient(
        projection_gradient_kernel,
        (*normed, *query_grads, *key_grads, *value_grads),
        tuple(shaped((width, columns)) for columns in (heads, HEAD, HEAD)),
        tuple(pl.BlockSpec((CHUNK, columns), lambda i: (i, 0)) for columns in (heads, HEAD, HEAD)),
        after,
    )


def output_gradient(grads, attended, after):
    heads, width = attended[0].shape[1], grads[0].shape[1]
    return weight_gradient(
        output_gradient_kernel,
        (*grads, *attended),
        (shaped((heads, width)), shaped((8, HEAD), jnp.float32)),
        (
            pl.BlockSpec((heads, CHUNK), lambda i: (0, i)),
            pl.BlockSpec((8, HEAD), lambda i: (0, 0)),
        ),
        after,
    )


def moved(x, route):
    count, lanes = lax.axis_size("pipe"), lax.axis_size("tensor")
    pairs = []
    for section in range(count):
        for lane in range(lanes):
            to_section, to_lane = route(section, lane)
            pairs.append((section * lanes + lane, to_section % count * lanes + to_lane))
    return lax.ppermute(x, ("pipe", "tensor"), pairs)


def around(lane, by):
    return lane // RING * RING + (lane + by) % RING


def across(x):
    return moved(x, lambda section, lane: (section, lane ^ RING))


def from_ahead(x):
    return [
        moved(x, lambda section, lane, by=by: (section, around(lane, -by)))
        for by in range(1, RING)
    ]


def to_ahead(xs):
    return [
        moved(x, lambda section, lane, by=by: (section, around(lane, by)))
        for by, x in enumerate(xs, 1)
    ]


def halve_shapes(near, riders):
    width = near.shape[1]
    piece = shaped((SHARD + riders, width))
    return (shaped((SHARD, width), jnp.float32),) + (piece,) * (RING - 1)


def quarter_shapes(terms):
    width, extra = terms[0].shape[1], terms[1].shape[1] - terms[0].shape[1]
    return shaped((SHARD, width), jnp.float32), shaped((SHARD, width + 2 * extra))


def sent_rows(place, stashed):
    _, _, _, width = stashed.shape
    return call(
        sent_rows_kernel,
        (shaped((2 * SHARD, width)),) * 2,
        (place, stashed),
        0,
        8 * SHARD * width,
        "sent_rows",
        SETUP_BYTES,
        specs={0: SCALAR, 1: AWAY},
        scratch=[pltpu.SemaphoreType.DMA((2, 2))],
    )


def set_up(place, tokens):
    table = shaped((tokens, HEAD), jnp.float32)
    out = call(
        setup_kernel,
        (table, table, shaped((tokens, tokens), jnp.float32), shaped(place.shape, jnp.int32)),
        (place, rope_tables(tokens)),
        tokens * HEAD,
        4 * tokens * HEAD,
        "setup",
        SMALL_BYTES,
        specs={0: SCALAR},
        last_scalar=True,
    )
    return out[:3], out[3]


def made_ready(table, weights):
    size = sum(w.size for w in weights)
    return call(
        ready_kernel, shaped(table.shape, jnp.float32), (table, *weights), 0, 2 * size,
        "weights_ready", LAYER_BYTES,
    )


def mirrored(rows):
    return moved(rows, lambda section, lane: (-1 - section, lane))


def per_device(
    forward_in,
    entering,
    backward_in,
    loss_grad,
    stashed,
    norm_gain,
    w_query,
    key_projection,
    value_projection,
    w_out,
):
    place = jnp.stack(
        [lax.axis_index("tensor"), lax.axis_index("pipe"), lax.axis_size("pipe") - 1]
    ).astype(jnp.int32)
    sent_pairs = sent_rows(place, stashed)
    tables, place = set_up(place, stashed.shape[2])
    weights = (w_query[0], key_projection[0], value_projection[0], w_out[0])
    tables = (made_ready(tables[0], weights), *tables[1:])
    gain = norm_gain
    own_in, own_grad = forward_in[0], backward_in[0]
    row = shaped(own_in.shape)
    both = shaped((2,) + row.shape)

    first_pair, second_pair = [mirrored(pair) for pair in sent_pairs]
    (in_pair,) = joined([(own_in, across(own_in))])
    in_pieces = (in_pair, *from_ahead(in_pair))
    grad_near, entering, loss_grad = joined(
        [(own_grad, *from_ahead(own_grad)), (entering,), (loss_grad,)], tables[0]
    )
    first_grads = (grad_near, across(grad_near))
    first_rows = (first_pair, *from_ahead(first_pair))
    first_terms = forward_term(in_pieces, gain, weights, tables)
    first_states = recomputed(first_rows, 0, gain, weights, tables)
    first_back_terms, first_grad_parts = backward_term(
        first_grads, first_states, weights, tables
    )
    own, *sent = small(
        halve_first_kernel, halve_shapes(first_terms[0], 2 * SHARD), first_terms[0],
        across(first_terms[1]), second_pair,
    )
    arrived = to_ahead(sent)
    second_rows = (second_pair, *arrived[::-1])
    first_out, handed_out = small(
        finish_forward_kernel, (row, row), in_pair, own, *arrived, place, entering,
        specs={5: SCALAR},
    )
    own, sent = small(
        quarter_first_kernel, quarter_shapes(first_back_terms),
        first_back_terms[0], *to_ahead(first_back_terms[1:]),
    )
    first_back, handed_back = small(
        finish_backward_kernel, (row, row), own, across(sent), first_states[0], grad_near, gain,
        place, loss_grad, specs={5: SCALAR},
    )

    next_pair, next_near = joined(
        [
            (
                moved(handed_out, lambda section, lane: (section + 1, lane)),
                moved(handed_out, lambda section, lane: (section + 1, lane ^ RING)),
            ),
            [
                moved(handed_back, lambda section, lane, by=by: (section - 1, around(lane, -by)))
                for by in range(RING)
            ],
        ]
    )
    next_pieces = (next_pair, *from_ahead(next_pair))
    second_grads = (next_near, across(next_near))
    second_states = recomputed(second_rows, SHARD, gain, weights, tables)
    second_terms = forward_term(next_pieces, gain, weights, tables, second_grads[1])
    second_back_terms, second_grad_parts = backward_term(
        second_grads, second_states, weights, tables, first_grad_parts[0]
    )
    grad_out, done = output_gradient(
        (*first_grads, *second_grads), (first_states[7], second_states[7]), second_grad_parts[0]
    )
    forward_own, *sent = small(
        halve_last_kernel, halve_shapes(second_terms[0], 0), second_terms[0],
        across(second_terms[1]), done, specs={2: ANYWHERE},
    )
    arrived = to_ahead(sent)
    forward_out = small(
        finish_forward_kernel, both, next_pair, forward_own, *arrived, first_out
    )
    own, sent, gain_sum = small(
        quarter_last_kernel,
        (*quarter_shapes(second_back_terms), shaped(second_grad_parts[0].shape, jnp.float32)),
        second_back_terms[0], *to_ahead(second_back_terms[1:]), second_grad_parts[0],
        *arrived, specs={RING + 1 + index: ANYWHERE for index in range(len(arrived))},
    )
    grad_query, key_weight_gradient, value_weight_gradient = projection_gradients(
        (first_states[1], second_states[1]),
        *[(first_grad_parts[index], second_grad_parts[index]) for index in (1, 2, 3)],
        own,
    )
    backward_out, grad_gain = small(
        finish_last_backward_kernel,
        (both, shaped(gain.shape, jnp.float32)),
        own, across(sent), second_states[0], next_near, gain, gain_sum, first_back,
    )
    return (
        forward_out[:, None],
        backward_out[:, None],
        grad_query[None],
        key_weight_gradient[None],
        value_weight_gradient[None],
        grad_out[None],
        grad_gain,
    )


def solution(mesh):
    in_specs = (
        P("pipe", "tensor", None),
        P("tensor", None),
        P("pipe", "tensor", None),
        P("tensor", None),
        P("pipe", None, None, None),
        P("pipe", None),
        P("pipe", None, "tensor"),
        P("pipe", None, "tensor"),
        P("pipe", None, "tensor"),
        P("pipe", "tensor", None),
    )
    out_specs = (
        P(None, "pipe", "tensor", None),
        P(None, "pipe", "tensor", None),
        P("pipe", None, "tensor"),
        P("pipe", None, "tensor"),
        P("pipe", None, "tensor"),
        P("pipe", "tensor", None),
        P("pipe", None),
    )
    return jax.shard_map(
        per_device, mesh=mesh, in_specs=in_specs, out_specs=out_specs, check_vma=False
    )
```
